32 devices in a mesh: replay: 4 (over y, core), mp: 8 (over z, x).
Axes of the slice: x: 2, y: 2, z: 4, core: 2. Of those that a mesh axis runs over, the one named last changes fastest.
Arguments:
- features: bfloat16 [1024, 32, 2048], P(('replay', 'mp')), may hold values from -40 to 40
- rewards: bfloat16 [1024, 32], P(('replay', 'mp')), may hold values from -32 to 32
- tail_value: bfloat16 [1024], P(('replay', 'mp')), may hold values from -12 to 12
- actions: int32 [1024, 32], P(('replay', 'mp')), may hold values from 0 to 1023
- episode_ends: int32 [1024, 32], P(('replay', 'mp')), may hold values 0 or 1
- sample_owner: int32 [1024, 1], P(('replay', 'mp')), may hold values from 0 to 3; in each aligned block of 32 rows (0 to 31, 32 to 63, ...) at most 8 rows name the same one
- sample_row: int32 [1024], P(('replay', 'mp')), may hold values from 0 to 31
- norm_gain: float32 [2048], replicated, may hold values from 0.1 to 1.9
- value_weight: bfloat16 [2048], replicated, may hold values from -0.125 to 0.125
- policy_weight: float32 [2048, 1024], P('mp'), may hold values from -1 to 1
- first_moment: float32 [2048, 1024], P('mp'), may hold values from -0.00048828125 to 0.00048828125
- second_moment: float32 [2048, 1024], P('mp'), may hold values from 2.9802323e-09 to 2.9802322e-08
Outputs:
- normalized_advantage: float32 [32768], P(('replay', 'mp'))
- update_direction: float32 [2048, 1024], P('mp')
- actor_policy: bfloat16 [2048, 1024], replicated
The draws below stay inside these ranges and needn't reach their ends.
Inputs may be any that keep to these rules, and one draw needn't show every extreme that they name: `sample_owner`: at most 8 of the 32 samples of one device name the same owner; exactly 8 do so on some devices.
All inputs are finite; a program needn't handle non-finite values. No bound on the sum of `episode_ends` on one device may be relied on, other than what follows from the above.
Results may differ from the reference program's by a relative error of at most 0.003.
Values may be sent and summed in bfloat16 or wider, within the bound.
No kernel may reach another device: no remote copies, remote signals or barrier semaphores. Data moves between devices by JAX's collectives and lax.ppermute only.
A program may use at most 128 MiB of HBM per device.

```python
import math
import jax
import jax.numpy as jnp
import numpy as np
from jax import lax

D = 2048
A = 1024
SEG = 32
SAMP = 32
SEGS_DEV = 32
CAP = 8
TOK_DEV = 1024
SAMPLES = 1024
TOKENS = 32768
SEGS_TOTAL = 1024
N_REPLAY = 4
N_MP = 8
DEVICES = 32


def draw_features(key, part):
    key = jax.random.fold_in(key, 1)
    first_key = jax.random.fold_in(key, 0)
    shape_all = (SEGS_TOTAL, SEG, D)
    drawn = jnp.clip(jax.random.normal(first_key, shape_all, jnp.float32), -4.0, 4.0)
    return drawn.astype(jnp.bfloat16)


def draw_rewards(key, part):
    key = jax.random.fold_in(key, 2)
    owner_device = jnp.arange(SEGS_TOTAL) // SEGS_DEV
    column_index = (owner_device % N_MP).astype(jnp.float32)
    scales = 1.0 + 2.0 * column_index / max(N_MP - 1, 1)
    drawn = jnp.clip(jax.random.normal(key, (SEGS_TOTAL, SEG), jnp.float32), -3.0, 3.0)
    return (scales[:, None] * (drawn + 0.5)).astype(jnp.bfloat16)


def draw_policy_weight(key, part):
    key = jax.random.fold_in(key, 3)
    scale_in = 1.0 / math.sqrt(D)
    drawn = jnp.clip(jax.random.normal(key, (D, A), jnp.float32), -4.0, 4.0) * scale_in
    return drawn


def plant(entries, stream_key, smallest, top_value):
    index_at = [jax.random.randint(jax.random.fold_in(stream_key, axis), (), 0, length) for axis, length in enumerate(entries.shape)]
    longest = entries.shape.index(max(entries.shape))
    neighbour = index_at[:longest] + [(index_at[longest] + 1) % entries.shape[longest]] + index_at[longest + 1:]
    return entries.at[tuple(index_at)].set(smallest).at[tuple(neighbour)].set(top_value)


def shard_levels(stream_key, shape, pieces, least, high):
    level = 1.0
    for axis_at, blocks in pieces:
        heights = jax.random.uniform(jax.random.fold_in(jax.random.fold_in(stream_key, 6), axis_at), (blocks,), jnp.float32, least / len(pieces), high / len(pieces))
        level = level * jnp.repeat(jnp.exp(heights), shape[axis_at] // blocks).reshape((-1,) + (1,) * (len(shape) - 1 - axis_at))
    return level


def routed_block(key, own, number, rows, amount, top, bound, lean):
    sequence = jax.random.permutation(key, amount)
    packed, usual = portions_of(amount, rows * top, bound, lean, True), portions_of(amount, rows * top, bound, lean, False)
    places = jnp.arange(amount)

    def named(sizes, turn):
        used = int((sizes > 0).sum())
        fixed = max(1, used // 4)
        moved = fixed + (places - fixed + turn * (used - fixed)) % max(1, amount - fixed)
        return jnp.zeros((amount,), jnp.int32).at[sequence[jnp.where(places < fixed, places, moved)]].set(jnp.asarray(sizes, jnp.int32))

    sizes = jnp.where(number % 4 == 0, named(packed, number // 4), named(usual, number - number // 4 - 1))
    mixed = jax.random.permutation(jax.random.fold_in(own, 3), amount)
    giver, taker = mixed[0:amount // 2 * 2:2], mixed[1:amount // 2 * 2:2]
    margin = jnp.minimum(sizes[giver] - 1, bound - sizes[taker]) // 2
    margin = jnp.where((giver == sequence[0]) | (taker == sequence[0]) | (sizes[taker] == 0), 0, jnp.maximum(margin, 0))
    moved = jax.random.randint(jax.random.fold_in(own, 4), (amount // 2,), 0, 1 << 20) % (margin + 1)
    sizes = sizes.at[giver].add(-moved).at[taker].add(moved)
    labels = jnp.searchsorted(jnp.cumsum(sizes), jnp.arange(rows * top), side="right").astype(jnp.int32)
    listing = labels.reshape(top, rows).T
    listing = listing[jax.random.permutation(jax.random.fold_in(own, 1), rows)]
    turn = jax.random.randint(jax.random.fold_in(own, 2), (rows, 1), 0, top)
    return jnp.take_along_axis(listing, (jnp.arange(top)[None, :] + turn) % top, axis=1)


def portions_of(amount, total, limit, lean, full):
    portions = [(1 << 20) // math.isqrt(rank ** lean) + 1 for rank in range(1, amount + 1)]
    largest = limit if full else min(limit, max(-(-total // amount), total * portions[0] // sum(portions)))
    least = 1 if total - largest >= amount - 1 else 0
    counts, surplus = [largest] + [least] * (amount - 1), total - largest - least * (amount - 1)
    while surplus > 0:
        free = [i for i in range(1, amount) if counts[i] < largest] or [i for i in range(1, amount) if counts[i] < limit]
        whole, budget = sum([portions[i] for i in free]), surplus
        for i in free:
            more = min(limit - counts[i], max(1, budget * portions[i] // whole), surplus)
            counts[i] = counts[i] + more
            surplus = surplus - more
    return np.array(counts)


def bell_draw(stream_key, extent, scale, bound, cuts=(), kind=jnp.bfloat16):
    values = scale * jax.random.normal(stream_key, extent, jnp.float32)
    if cuts:
        values = values * shard_levels(stream_key, extent, cuts, -0.22, 0.18)
    return jnp.clip(values, -bound, bound).astype(kind)


def setup_inputs(seed: int = 0) -> dict:
    key_list = jax.random.split(jax.random.key(seed), 13)
    features = draw_features(jax.random.fold_in(key_list[12], 71), 0)
    rewards = draw_rewards(jax.random.fold_in(key_list[12], 71), 0)
    tail_value = bell_draw(key_list[2], (SEGS_TOTAL,), 3.0, 12.0, ((0, 32),))
    actions = plant(jax.random.randint(key_list[3], (SEGS_TOTAL, SEG), 0, A), jax.random.fold_in(key_list[3], 1), 0, A - 1).astype(jnp.int32)
    episode_ends = plant((jax.random.randint(key_list[4], (SEGS_TOTAL, SEG), 0, 8) < 1).astype(jnp.int32), jax.random.fold_in(key_list[4], 1), 0, 1)
    sample_owner_keys = jax.random.split(jax.random.fold_in(key_list[5], 1), SAMPLES // SAMP)
    sample_owner_turns = jax.random.permutation(jax.random.fold_in(key_list[5], 3), SAMPLES // SAMP)
    sample_owner = jax.vmap(lambda own, number: routed_block(jax.random.fold_in(key_list[5], 2), own, number, SAMP, N_REPLAY, 1, CAP, 2))(sample_owner_keys, sample_owner_turns).reshape((SAMPLES, 1))
    sample_row = plant(jax.random.randint(key_list[6], (SAMPLES,), 0, SEGS_DEV), jax.random.fold_in(key_list[6], 1), 0, SEGS_DEV - 1).astype(jnp.int32)
    norm_gain = jnp.clip(1.0 + 0.18 * jax.random.normal(key_list[7], (D,), jnp.float32), 0.1, 1.9)
    value_weight = bell_draw(key_list[8], (D,), D ** -0.5, 0.125)
    policy_weight = draw_policy_weight(jax.random.fold_in(key_list[12], 71), 0)
    first_moment = bell_draw(key_list[10], (D, A), (0.5 * (TOKENS * A) ** -0.5), 0.00048828125, ((0, 8),), jnp.float32)
    second_moment = jnp.clip(jnp.exp(math.log(2.9802322387695312e-08) - 2.3025851 * jax.random.uniform(key_list[11], (D, A), jnp.float32) ** shard_levels(key_list[11], (D, A), ((0, 8),), -0.2, 0.2)), 2.9802322831784522e-09, 2.9802322387695312e-08)
    return dict(features=features, rewards=rewards, tail_value=tail_value, actions=actions, episode_ends=episode_ends, sample_owner=sample_owner, sample_row=sample_row, norm_gain=norm_gain, value_weight=value_weight, policy_weight=policy_weight, first_moment=first_moment, second_moment=second_moment)


DISCOUNT = 0.97
STEP_RATE = 0.002

def normalize(rows, norm_gain):
    widened = rows.astype(jnp.float32)
    mean_square = lax.optimization_barrier(jnp.mean(widened * widened, axis=-1, keepdims=True))
    return (widened * lax.rsqrt(mean_square + 1e-05) * norm_gain).astype(jnp.bfloat16)

def discount(step_rewards, step_ends, tail_values):

    def backward(carried, inputs):
        reward_now, end_now = inputs
        carried = reward_now + DISCOUNT * (1.0 - end_now.astype(jnp.float32)) * carried
        return (carried, carried)
    _, stacked = lax.scan(backward, tail_values, (step_rewards.T, step_ends.T), reverse=True)
    return stacked.T

def reference(features, rewards, tail_value, actions, episode_ends, sample_owner, sample_row, norm_gain, value_weight, policy_weight, first_moment, second_moment):
    learner = jnp.arange(SAMPLES, dtype=jnp.int32) // SAMP
    segment = ((sample_owner[:, 0] * N_MP + learner % N_MP) * SEGS_DEV + sample_row).astype(jnp.int32)
    blocks = segment.reshape(DEVICES, SAMP)

    def block_normed(indices):
        return normalize(features[indices], norm_gain).reshape(TOK_DEV, D)

    def block_values(indices):
        return jnp.dot(block_normed(indices), value_weight, preferred_element_type=jnp.float32)
    values = lax.map(block_values, blocks).reshape(TOKENS)
    step_rewards = rewards[segment].astype(jnp.float32)
    step_ends = episode_ends[segment]
    tail_values = tail_value[segment].astype(jnp.float32)
    returns = discount(step_rewards, step_ends, tail_values).reshape(TOKENS)
    advantage = returns - values
    mean_adv = jnp.sum(advantage) / TOKENS
    centered = advantage - mean_adv
    spread = jnp.sum(centered * centered) / TOKENS
    normalized = centered * lax.rsqrt(spread + 1e-05)
    weights = jnp.exp(jnp.minimum(normalized, 3.0))
    total_weight = jnp.sum(weights)
    policy_low = policy_weight.astype(jnp.bfloat16)
    step_actions = actions[segment].reshape(DEVICES, TOK_DEV)
    contract = (((0,), (0,)), ((), ()))

    def accumulate(carried, inputs):
        indices, block_weights, block_actions = inputs
        normed = block_normed(indices)
        logits = jnp.dot(normed, policy_low, preferred_element_type=jnp.float32)
        row_top = lax.optimization_barrier(jnp.max(logits, axis=1, keepdims=True))
        shifted = logits - row_top
        chances = jnp.exp(shifted - jnp.log(lax.optimization_barrier(jnp.sum(jnp.exp(shifted), axis=1, keepdims=True))))
        chosen = (block_actions[:, None] == jnp.arange(A, dtype=jnp.int32)[None, :]).astype(jnp.float32)
        signal = (block_weights[:, None] * (chances - chosen)).astype(jnp.bfloat16)
        return (carried + lax.dot_general(normed, signal, contract, preferred_element_type=jnp.float32), None)
    gradient_sum, _ = lax.scan(accumulate, jnp.zeros((D, A), jnp.float32), (blocks, weights.reshape(DEVICES, TOK_DEV), step_actions))
    gradient = gradient_sum / total_weight
    first_new = 0.9 * first_moment + 0.1 * gradient
    second_new = 0.95 * second_moment + 0.05 * gradient * gradient
    update = first_new / (jnp.sqrt(second_new) + 1e-08)
    actor_policy = (policy_weight - STEP_RATE * update).astype(jnp.bfloat16)
    return (normalized, update, actor_policy)
```

```python
import functools

import jax
import jax.numpy as jnp
from jax import lax
from jax.experimental import pallas as pl
from jax.experimental.pallas import tpu as pltpu
from jax.sharding import PartitionSpec as P

DISCOUNT = 0.97
STEP_RATE = 0.002
ALL = ("replay", "mp")
LANES = 128
BF16 = jnp.bfloat16
F32 = jnp.float32
VMEM = pl.BlockSpec(memory_space=pltpu.VMEM)
SMEM = pl.BlockSpec(memory_space=pltpu.SMEM)
ANY = pl.BlockSpec(memory_space=pl.ANY)


class Plan:
    def __init__(self, replay, mp, actions):
        self.C = 2
        self.Y = replay // self.C
        self.Z = 4
        self.X = mp // self.Z
        self.mp = mp
        self.swap = self.X == self.Y
        self.block = LANES
        self.J = max(1, actions // (self.C * self.Y * self.block))

    def permute(self, value, axis, k):
        pairs = []
        for y in range(self.Y):
            for c in range(self.C):
                for z in range(self.Z):
                    for x in range(self.X):
                        along = axis
                        if axis in ("p", "q"):
                            along = "y" if (axis == "p") == (c == 0 or not self.swap) else "x"
                        to = dict(y=y, c=c, z=z, x=x)
                        to[along] ^= k
                        pairs.append((self.index(y, c, z, x), self.index(**to)))
        return lax.ppermute(value, ALL, pairs)

    def index(self, y, c, z, x):
        return (y * self.C + c) * self.mp + z * self.X + x

    def here(self):
        replay, mp = lax.axis_index("replay"), lax.axis_index("mp")
        return jnp.stack([replay // self.C, replay % self.C, mp // self.X, mp % self.X]).astype(jnp.int32)

    def relative(self, core, dy, dx):
        if not self.swap:
            return dy, dx
        return jnp.where(core == 0, dy, dx), jnp.where(core == 0, dx, dy)

    def gather_column(self, block):
        return jnp.stack([block] + [self.permute(block, "z", k) for k in range(1, self.Z)])

    def gather_rest(self, column):
        plane = jnp.stack([column] + [self.permute(column, "q", k) for k in range(1, self.X)])
        mine = [plane] + [self.permute(plane, "p", k) for k in range(1, self.Y)]
        return mine + [self.permute(piece, "c", 1) for piece in mine]

    def reduce(self, keep, send):
        total = keep + self.permute(send, "c", 1).astype(F32)
        for axis in ("p", "q", "z"):
            low = total[1:].astype(BF16)
            total = total[0]
            terms = [self.permute(low[k - 1], axis, k) for k in range(1, low.shape[0] + 1)]
            if axis == "z":
                return total, terms
            for term in terms:
                total = total + term.astype(F32)


def shard_kernel(place_ref, w_ref, out_ref):
    out_ref[0] = w_ref[...].T.astype(BF16)


def own_shard(plan, place, policy_weight):
    depth = policy_weight.shape[0]
    block = plan.block
    return pl.pallas_call(
        shard_kernel,
        grid_spec=pltpu.PrefetchScalarGridSpec(
            num_scalar_prefetch=1,
            grid=(plan.J,),
            in_specs=[pl.BlockSpec((depth, block), lambda j, place: (0, j * 2 * plan.Y + place[0]))],
            out_specs=pl.BlockSpec((1, block, depth), lambda j, place: (j, 0, 0)),
        ),
        out_shape=jax.ShapeDtypeStruct((plan.J, block, depth), BF16),
        name="shard",
    )(place, policy_weight)


def update_kernel(count, place_ref, mass_ref, base_ref, *refs):
    terms, (w_ref, m_ref, v_ref, update_ref, low_ref) = refs[:count], refs[count:]
    total = base_ref[...]
    for term in terms:
        total = total + term[...].astype(F32)
    gradient = total.T / mass_ref[0, 0]
    first_new = 0.9 * m_ref[...] + 0.1 * gradient
    second_new = 0.95 * v_ref[...] + 0.05 * gradient * gradient
    update = first_new / (jnp.sqrt(second_new) + 1e-08)
    update_ref[...] = update
    low_ref[...] = (w_ref[...] - STEP_RATE * update).astype(BF16)


def own_update(plan, j, place, mass, base, terms, policy_weight, first_moment, second_moment):
    depth = policy_weight.shape[0]
    block = plan.block
    whole = pl.BlockSpec((block, depth), lambda i, place: (0, 0))
    own = pl.BlockSpec((depth, block), lambda i, place: (0, j * 2 * plan.Y + place[0]))
    out = pl.BlockSpec((depth, block), lambda i, place: (0, 0))
    return pl.pallas_call(
        functools.partial(update_kernel, len(terms)),
        grid_spec=pltpu.PrefetchScalarGridSpec(
            num_scalar_prefetch=1,
            grid=(1,),
            in_specs=[SMEM, whole] + [whole] * len(terms) + [own] * 3,
            out_specs=[out, out],
        ),
        out_shape=[
            jax.ShapeDtypeStruct((depth, block), F32),
            jax.ShapeDtypeStruct((depth, block), BF16),
        ],
        name="update",
    )(place, mass, base, *terms, policy_weight, first_moment, second_moment)


def norm_kernel(x_ref, gain_ref, value_ref, out_ref, val_ref):
    wide = x_ref[...].astype(F32)
    mean_square = jnp.mean(wide * wide, axis=-1, keepdims=True)
    normed = (wide * lax.rsqrt(mean_square + 1e-05) * gain_ref[...]).astype(BF16)
    out_ref[...] = normed
    val_ref[...] = lax.dot_general(
        value_ref[...], normed, (((1,), (1,)), ((), ())), preferred_element_type=F32
    )


def normalize(rows, norm_gain, value_weight):
    tokens, width = rows.shape
    tile = 256
    normed, values = pl.pallas_call(
        norm_kernel,
        grid=(tokens // tile,),
        in_specs=[
            pl.BlockSpec((tile, width), lambda i: (i, 0)),
            pl.BlockSpec((1, width), lambda i: (0, 0)),
            pl.BlockSpec((16, width), lambda i: (0, 0)),
        ],
        out_specs=[
            pl.BlockSpec((tile, width), lambda i: (i, 0)),
            pl.BlockSpec((16, tile), lambda i: (0, i)),
        ],
        out_shape=[
            jax.ShapeDtypeStruct((tokens, width), BF16),
            jax.ShapeDtypeStruct((16, tokens), F32),
        ],
        compiler_params=pltpu.CompilerParams(vmem_limit_bytes=32 * 2**20),
        cost_estimate=pl.CostEstimate(
            flops=10 * tokens * width, bytes_accessed=4 * tokens * width, transcendentals=0
        ),
        name="normalize",
    )(rows, norm_gain.reshape(1, width), jnp.broadcast_to(value_weight[None, :], (16, width)))
    return normed, values[0]


def advantage_kernel(seg_len, r_ref, e_ref, tail_ref, v_ref, out_ref):
    lane = lax.broadcasted_iota(jnp.int32, r_ref.shape, 1) % seg_len
    last = lane == seg_len - 1
    decay = DISCOUNT * (1.0 - e_ref[...])
    total = r_ref[...] + jnp.where(last, decay * tail_ref[...], 0.0)
    decay = jnp.where(last, 0.0, decay)
    reach = 1
    while reach < seg_len:
        total = total + decay * pltpu.roll(total, LANES - reach, axis=1)
        decay = decay * pltpu.roll(decay, LANES - reach, axis=1)
        reach *= 2
    out_ref[...] = total - v_ref[...]


def advantages(rewards, ends, tails, values):
    segs, seg_len = rewards.shape
    shape = (segs * seg_len // LANES, LANES)
    tails = jnp.broadcast_to(tails.astype(F32)[:, None], rewards.shape)
    return pl.pallas_call(
        functools.partial(advantage_kernel, seg_len),
        in_specs=[VMEM] * 4,
        out_specs=VMEM,
        out_shape=jax.ShapeDtypeStruct(shape, F32),
        name="advantage",
    )(
        rewards.astype(F32).reshape(shape),
        ends.astype(F32).reshape(shape),
        tails.reshape(shape),
        values.reshape(shape),
    )


def gradient_chunk(plan, j, here, sig_ref, n_ref, keep_ref, send_ref):
    y, c, z, x = here
    rows = plan.Y * plan.block
    depth = keep_ref.shape[-1]

    def step(m, carry):
        start = pl.multiple_of(m * depth, depth)
        part = jnp.dot(
            sig_ref[j * 2 * rows : (j + 1) * 2 * rows, :],
            n_ref[:, pl.ds(start, depth)],
            preferred_element_type=F32,
        )
        first, second = part[:rows], part[rows:]
        keep = jnp.where(c == 0, first, second)
        send = jnp.where(c == 0, second, first).astype(BF16)
        dz, dx = (m // plan.X) ^ z, (m % plan.X) ^ x
        for col in range(plan.Y):
            p, q = plan.relative(c, y ^ col, dx)
            keep_ref[p, q, dz] = keep[col * plan.block : (col + 1) * plan.block]
            p, q = plan.relative(1 - c, y ^ col, dx)
            send_ref[p, q, dz] = send[col * plan.block : (col + 1) * plan.block]
        return carry

    lax.fori_loop(0, plan.mp, step, 0)


def signal_kernel(plan, here_ref, w_ref, act_ref, *refs):
    count = plan.J * 2 * plan.Y
    pieces, refs = refs[:count], refs[count:]
    n_hbm, sig_ref, keep_ref, send_ref, wt_ref, n_ref, l_ref, w_sems, n_sem = refs
    y, c, z, x = here = tuple(here_ref[i] for i in range(4))
    depth = keep_ref.shape[-1]
    block = plan.block
    n_copy = pltpu.make_async_copy(n_hbm, n_ref, n_sem)
    n_copy.start()
    copies = []
    for j in range(plan.J):
        for other in range(2):
            core = c ^ other
            for p in range(plan.Y):
                piece = pieces[(j * 2 + other) * plan.Y + p]
                for q in range(plan.X):
                    a, b = plan.relative(core, p, q)
                    for dz in range(plan.Z):
                        row = ((j * 2 + core) * plan.Y + (y ^ a)) * block
                        col = ((z ^ dz) * plan.X + (x ^ b)) * depth
                        copy = pltpu.make_async_copy(
                            piece.at[q, dz],
                            wt_ref.at[pl.ds(pl.multiple_of(row, block), block), pl.ds(pl.multiple_of(col, depth), depth)],
                            w_sems.at[len(copies)],
                        )
                        copy.start()
                        copies.append(copy)
    n_copy.wait()
    for copy in copies:
        copy.wait()
    actions, tokens = sig_ref.shape
    tile = l_ref.shape[1]
    group = 256

    def step(t, carry):
        where = pl.ds(pl.multiple_of(t * tile, tile), tile)
        normed = n_ref[where, :]
        top = None
        for a in range(actions // group):
            part = lax.dot_general(
                wt_ref[a * group : (a + 1) * group, :],
                normed,
                (((1,), (1,)), ((), ())),
                preferred_element_type=F32,
            )
            l_ref[a * group : (a + 1) * group, :] = part
            high = jnp.max(part, axis=0, keepdims=True)
            top = high if top is None else jnp.maximum(top, high)
        mass = jnp.zeros_like(top)
        for a in range(actions // group):
            part = jnp.exp(l_ref[a * group : (a + 1) * group, :] - top)
            l_ref[a * group : (a + 1) * group, :] = part
            mass = mass + jnp.sum(part, axis=0, keepdims=True)
        weight = w_ref[:, where]
        chosen = act_ref[:, where]
        inverse = 1.0 / mass
        for a in range(actions // group):
            row = lax.broadcasted_iota(jnp.int32, (group, tile), 0) + a * group
            chance = l_ref[a * group : (a + 1) * group, :] * inverse
            part = weight * (chance - jnp.where(row == chosen, 1.0, 0.0))
            sig_ref[a * group : (a + 1) * group, where] = part.astype(BF16)
        return carry

    lax.fori_loop(0, tokens // tile, step, 0)
    gradient_chunk(plan, 0, here, sig_ref, n_ref, keep_ref, send_ref)


def gradient_kernel(plan, j, here_ref, sig_ref, n_ref, keep_ref, send_ref):
    gradient_chunk(plan, j, tuple(here_ref[i] for i in range(4)), sig_ref, n_ref, keep_ref, send_ref)


def chunk_shapes(plan, depth):
    shape = (plan.Y, plan.X, plan.Z, plan.block, depth)
    return [jax.ShapeDtypeStruct(shape, F32), jax.ShapeDtypeStruct(shape, BF16)]


def signal_and_gradient(plan, here, weights, actions, pieces, normed, count):
    tokens, width = normed.shape
    depth = width // plan.mp
    sig, keep, send = pl.pallas_call(
        functools.partial(signal_kernel, plan),
        in_specs=[SMEM, VMEM, VMEM] + [ANY] * (len(pieces) + 1),
        out_specs=[VMEM] * 3,
        out_shape=[jax.ShapeDtypeStruct((count, tokens), BF16)] + chunk_shapes(plan, depth),
        scratch_shapes=[
            pltpu.VMEM((count, width), BF16),
            pltpu.VMEM((tokens, width), BF16),
            pltpu.VMEM((count, 256), F32),
            pltpu.SemaphoreType.DMA((len(pieces) * plan.X * plan.Z,)),
            pltpu.SemaphoreType.DMA,
        ],
        compiler_params=pltpu.CompilerParams(vmem_limit_bytes=48 * 2**20),
        cost_estimate=pl.CostEstimate(
            flops=2 * tokens * width * count * (plan.J + 1) // plan.J,
            bytes_accessed=2 * tokens * width + 2 * width * count + 2 * tokens * count,
            transcendentals=tokens * count,
        ),
        name="signal",
    )(here, weights, actions, *pieces, normed)
    chunks = [(keep, send)]
    for j in range(1, plan.J):
        chunks.append(
            pl.pallas_call(
                functools.partial(gradient_kernel, plan, j),
                in_specs=[SMEM, VMEM, VMEM],
                out_specs=[VMEM] * 2,
                out_shape=chunk_shapes(plan, depth),
                compiler_params=pltpu.CompilerParams(vmem_limit_bytes=48 * 2**20),
                cost_estimate=pl.CostEstimate(
                    flops=2 * tokens * width * count // plan.J,
                    bytes_accessed=2 * tokens * width + 2 * tokens * count,
                    transcendentals=0,
                ),
                name="gradient",
            )(here, sig, normed)
        )
    return chunks


def assemble_kernel(plan, here_ref, *refs):
    count = plan.J * 2 * plan.Y
    pieces = refs[:count]
    near, far, actor_ref, update_ref, sems = refs[count:]
    y, c, z, x = (here_ref[i] for i in range(4))
    depth = near.shape[-2]
    block = plan.block
    copies = []

    def copy(source, target):
        moved = pltpu.make_async_copy(source, target, sems.at[len(copies)])
        moved.start()
        copies.append(moved)

    for j in range(plan.J):
        for other in range(2):
            core = c ^ other
            for dy in range(plan.Y):
                col = ((j * 2 + core) * plan.Y + (y ^ dy)) * block
                copy(
                    (far if other else near).at[dy, j],
                    update_ref.at[:, pl.ds(pl.multiple_of(col, block), block)],
                )
            for p in range(plan.Y):
                piece = pieces[(j * 2 + other) * plan.Y + p]
                for q in range(plan.X):
                    a, b = plan.relative(core, p, q)
                    for dz in range(plan.Z):
                        col = ((j * 2 + core) * plan.Y + (y ^ a)) * block
                        row = ((z ^ dz) * plan.X + (x ^ b)) * depth
                        copy(
                            piece.at[q, dz],
                            actor_ref.at[pl.ds(pl.multiple_of(row, depth), depth), pl.ds(pl.multiple_of(col, block), block)],
                        )
    for moved in copies:
        moved.wait()


def assemble(plan, here, pieces, near, far, width, count):
    depth = width // plan.mp
    return pl.pallas_call(
        functools.partial(assemble_kernel, plan),
        in_specs=[SMEM] + [VMEM] * (len(pieces) + 2),
        out_specs=[ANY] * 2,
        out_shape=[
            jax.ShapeDtypeStruct((width, count), BF16),
            jax.ShapeDtypeStruct((depth, count), F32),
        ],
        scratch_shapes=[
            pltpu.SemaphoreType.DMA((len(pieces) * plan.X * plan.Z + plan.J * 2 * plan.Y,)),
        ],
        compiler_params=pltpu.CompilerParams(vmem_limit_bytes=32 * 2**20),
        name="assemble",
    )(here, *pieces, near, far)


def body(
    features,
    rewards,
    tail_value,
    actions,
    episode_ends,
    sample_owner,
    sample_row,
    norm_gain,
    value_weight,
    policy_weight,
    first_moment,
    second_moment,
):
    owners_all, columns = lax.axis_size("replay"), lax.axis_size("mp")
    segs, seg_len, width = features.shape
    depth, count = policy_weight.shape
    samples = sample_row.shape[0]
    plan = Plan(owners_all, columns, count)
    here = plan.here()
    place = (here[1] * plan.Y + here[0]).reshape(1)
    replay = lax.axis_index("replay")

    low = own_shard(plan, place, policy_weight)
    stages = [plan.gather_column(low[j]) for j in range(plan.J)]
    stages[0], norm_gain = lax.optimization_barrier((stages[0], norm_gain))
    pieces = [piece for column in stages for piece in plan.gather_rest(column)]

    normed, values = normalize(features.reshape(segs * seg_len, width), norm_gain, value_weight)
    advantage = advantages(rewards, episode_ends, tail_value, values)

    rows = advantage.shape[0]
    request = (sample_owner[:, 0] * segs + sample_row).astype(F32)
    request = jnp.pad(request[None, :], ((0, 7), (0, LANES - samples)))
    known = jnp.concatenate([advantage, request])
    for axis, size in (("z", plan.Z), ("x", plan.X), ("y", plan.Y), ("c", plan.C)):
        known = jnp.stack([known] + [plan.permute(known, axis, k) for k in range(1, size)])
    lead = (plan.C, plan.Y, plan.X, plan.Z)
    advantage = known[..., :rows, :].reshape(lead + (segs, seg_len))
    request = known[..., rows, :samples].astype(jnp.int32)
    code = (request // segs ^ replay) * segs + request % segs
    marks = jnp.transpose(code, (2, 3, 0, 1, 4)).reshape(plan.X, plan.Z, -1)
    slots = jnp.arange(owners_all * segs, dtype=jnp.int32)
    times = jnp.sum((marks[..., None] == slots).astype(F32), axis=2)
    times = times.reshape(plan.X, plan.Z, plan.Y, plan.C, segs)
    times = jnp.transpose(times, (3, 2, 0, 1, 4))[..., None]

    token_total = owners_all * columns * samples * seg_len
    centered = advantage - jnp.sum(times * advantage) / token_total
    spread = jnp.sum(times * centered * centered) / token_total
    normalized = centered * lax.rsqrt(spread + 1e-05)
    weights = times * jnp.exp(jnp.minimum(normalized, 3.0))
    total_weight = jnp.sum(weights)
    column = jnp.transpose(normalized[:, :, 0, 0], (1, 0, 2, 3)).reshape(owners_all * segs, seg_len)
    local_norm = column[code[0, 0, 0, 0]].reshape(-1)

    chunks = signal_and_gradient(
        plan,
        here,
        weights[0, 0, 0, 0].reshape(1, -1),
        actions.reshape(1, -1),
        pieces,
        normed,
        count,
    )
    updates, fresh = [], []
    for j, (keep, send) in enumerate(chunks):
        base, terms = plan.reduce(keep, send)
        update, low = own_update(
            plan, j, place, total_weight.reshape(1, 1), base, terms, policy_weight, first_moment, second_moment
        )
        updates.append(update)
        fresh += plan.gather_rest(plan.gather_column(low))
    near = jnp.stack(updates)
    near = jnp.stack([near] + [plan.permute(near, "y", k) for k in range(1, plan.Y)])
    far = plan.permute(near, "c", 1)
    actor_policy, update = assemble(plan, here, fresh, near, far, width, count)
    return (local_norm, update, actor_policy)


def solution(mesh):
    return jax.shard_map(
        body,
        mesh=mesh,
        in_specs=(
            P(ALL, None, None),
            P(ALL, None),
            P(ALL),
            P(ALL, None),
            P(ALL, None),
            P(ALL, None),
            P(ALL),
            P(),
            P(),
            P("mp", None),
            P("mp", None),
            P("mp", None),
        ),
        out_specs=(P(ALL), P("mp", None), P()),
        check_vma=False,
    )
```

```python
import functools

import jax
import jax.numpy as jnp
from jax import lax
from jax.experimental import pallas as pl
from jax.experimental.pallas import tpu as pltpu
from jax.sharding import PartitionSpec as P

DISCOUNT = 0.97
STEP_RATE = 0.002
ALL = ("replay", "mp")
LANES = 128
BF16 = jnp.bfloat16
F32 = jnp.float32
VMEM = pl.BlockSpec(memory_space=pltpu.VMEM)
SMEM = pl.BlockSpec(memory_space=pltpu.SMEM)
ANY = pl.BlockSpec(memory_space=pl.ANY)
ROOM = pltpu.CompilerParams(vmem_limit_bytes=32 * 2**20)


class Plan:
    def __init__(self, replay, mp, actions):
        self.C = 2
        self.Y = replay // self.C
        self.Z = 4
        self.X = mp // self.Z
        self.mp = mp
        self.swap = self.X == self.Y
        self.block = LANES
        self.J = max(1, actions // (self.C * self.Y * self.block))

    def permute(self, value, axis, k):
        pairs = []
        for y in range(self.Y):
            for c in range(self.C):
                for z in range(self.Z):
                    for x in range(self.X):
                        along = axis
                        if axis in ("p", "q"):
                            along = "y" if (axis == "p") == (c == 0 or not self.swap) else "x"
                        to = dict(y=y, c=c, z=z, x=x)
                        to[along] ^= k
                        pairs.append((self.index(y, c, z, x), self.index(**to)))
        return lax.ppermute(value, ALL, pairs)

    def index(self, y, c, z, x):
        return (y * self.C + c) * self.mp + z * self.X + x

    def here(self):
        replay, mp = lax.axis_index("replay"), lax.axis_index("mp")
        return jnp.stack([replay // self.C, replay % self.C, mp // self.X, mp % self.X]).astype(jnp.int32)

    def relative(self, core, dy, dx):
        if not self.swap:
            return dy, dx
        return jnp.where(core == 0, dy, dx), jnp.where(core == 0, dx, dy)

    def gather_column(self, block):
        return [block] + [self.permute(block, "z", k) for k in range(1, self.Z)]

    def gather_rest(self, column):
        column = jnp.stack(column)
        plane = jnp.stack([column] + [self.permute(column, "q", k) for k in range(1, self.X)])
        mine = [plane] + [self.permute(plane, "p", k) for k in range(1, self.Y)]
        return mine + [self.permute(piece, "c", 1) for piece in mine]

    def reduce(self, keep, send):
        total = keep + self.permute(send, "c", 1).astype(F32)
        for axis in ("p", "q"):
            low = total[1:].astype(BF16)
            total = total[0]
            for k in range(1, low.shape[0] + 1):
                total = total + self.permute(low[k - 1], axis, k).astype(F32)
        return total[0], [total[k].astype(BF16) for k in range(1, self.Z)]

    def reduce_column(self, low):
        return [self.permute(low[k - 1], "z", k) for k in range(1, self.Z)]


def shard_kernel(plan, place_ref, w_hbm, *refs):
    outs, stage, sems = refs[: plan.J], refs[plan.J], refs[plan.J + 1]
    block = plan.block
    copies = []
    for j in range(plan.J):
        start = pl.multiple_of((j * 2 * plan.Y + place_ref[0]) * block, block)
        copy = pltpu.make_async_copy(w_hbm.at[:, pl.ds(start, block)], stage.at[j], sems.at[j])
        copy.start()
        copies.append(copy)
    for j in range(plan.J):
        copies[j].wait()
        outs[j][...] = stage[j].T.astype(BF16)


def own_shard(plan, place, policy_weight):
    depth = policy_weight.shape[0]
    block = plan.block
    return pl.pallas_call(
        functools.partial(shard_kernel, plan),
        in_specs=[SMEM, ANY],
        out_specs=[VMEM] * plan.J,
        out_shape=[jax.ShapeDtypeStruct((block, depth), BF16)] * plan.J,
        scratch_shapes=[pltpu.VMEM((plan.J, depth, block), F32), pltpu.SemaphoreType.DMA((plan.J,))],
        name="shard",
    )(place, policy_weight)


def update_kernel(count, place_ref, mass_ref, base_ref, *refs):
    terms, (w_ref, m_ref, v_ref, update_ref, low_ref) = refs[:count], refs[count:]
    total = base_ref[...]
    for term in terms:
        total = total + term[...].astype(F32)
    gradient = total.T / mass_ref[0, 0]
    first_new = 0.9 * m_ref[...] + 0.1 * gradient
    second_new = 0.95 * v_ref[...] + 0.05 * gradient * gradient
    update = first_new / (jnp.sqrt(second_new) + 1e-08)
    update_ref[...] = update
    low_ref[...] = (w_ref[...] - STEP_RATE * update).astype(BF16)


def own_update(plan, j, place, mass, base, terms, policy_weight, first_moment, second_moment):
    depth = policy_weight.shape[0]
    block = plan.block
    whole = pl.BlockSpec((block, depth), lambda i, place: (0, 0))
    own = pl.BlockSpec((depth, block), lambda i, place: (0, j * 2 * plan.Y + place[0]))
    out = pl.BlockSpec((depth, block), lambda i, place: (0, 0))
    return pl.pallas_call(
        functools.partial(update_kernel, len(terms)),
        grid_spec=pltpu.PrefetchScalarGridSpec(
            num_scalar_prefetch=1,
            grid=(1,),
            in_specs=[SMEM, whole] + [whole] * len(terms) + [own] * 3,
            out_specs=[out, out],
        ),
        out_shape=[
            jax.ShapeDtypeStruct((depth, block), F32),
            jax.ShapeDtypeStruct((depth, block), BF16),
        ],
        name="update",
    )(place, mass, base, *terms, policy_weight, first_moment, second_moment)


def spread_rows(rows, lanes):
    n, steps = rows.shape
    lane = lax.broadcasted_iota(jnp.int32, (steps, lanes), 1)
    pick = (lane % steps == lax.broadcasted_iota(jnp.int32, (steps, lanes), 0)).astype(F32).astype(BF16)
    wide = jnp.dot(rows.astype(BF16), pick, preferred_element_type=F32)
    lane = lax.broadcasted_iota(jnp.int32, (n, lanes), 1)
    own = lane // steps == lax.broadcasted_iota(jnp.int32, (n, lanes), 0)
    return jnp.sum(jnp.where(own, wide, 0.0), axis=0, keepdims=True)


def norm_kernel(x_ref, gain_ref, value_ref, r_ref, e_ref, tail_ref, ask_ref, low_ref, out_ref, block_ref, val_ref):
    wide = x_ref[...].astype(F32)
    mean_square = jnp.mean(wide * wide, axis=-1, keepdims=True)
    normed = (wide * lax.rsqrt(mean_square + 1e-05) * gain_ref[...]).astype(BF16)
    out_ref[...] = normed
    tile = normed.shape[0]
    step = pl.program_id(0)
    val_ref[:, pl.ds(pl.multiple_of(step * tile, tile), tile)] = lax.dot_general(
        value_ref[...], normed, (((1,), (1,)), ((), ())), preferred_element_type=F32
    )

    @pl.when(step == pl.num_programs(0) - 1)
    def _():
        segs, seg_len = r_ref.shape
        lanes = segs * seg_len
        lane = lax.broadcasted_iota(jnp.int32, (1, lanes), 1)
        last = lane % seg_len == seg_len - 1
        ends = spread_rows(e_ref[...].astype(F32), lanes)
        tails = spread_rows(jnp.broadcast_to(tail_ref[...].astype(F32), (segs, seg_len)), lanes)
        decay = DISCOUNT * (1.0 - ends)
        total = spread_rows(r_ref[...], lanes) + jnp.where(last, decay * tails, 0.0)
        decay = jnp.where(last, 0.0, decay)
        reach = 1
        while reach < seg_len:
            total = total + decay * pltpu.roll(total, lanes - reach, axis=1)
            decay = decay * pltpu.roll(decay, lanes - reach, axis=1)
            reach *= 2
        rest = total - val_ref[0:1, :]
        block, depth = low_ref.shape
        rows = []
        for _ in range(3):
            term = rest.astype(BF16).astype(F32)
            rest = rest - term
            rows += [term[:, i : i + depth] for i in range(0, lanes, depth)]
        rows.append(ask_ref[...])
        rows.append(jnp.zeros((block_ref.shape[0] - block - len(rows), depth), F32))
        block_ref[:block, :] = low_ref[...]
        block_ref[block:, :] = jnp.concatenate(rows, axis=0).astype(BF16)


def payload_rows(lanes, depth):
    return -(-(3 * lanes // depth + 1) // 16) * 16


def normalize(rows, norm_gain, value_weight, rewards, ends, tails, asked, low):
    tokens, width = rows.shape
    tile = 256
    block, depth = low.shape
    segs = tails.shape[0]
    high = block + payload_rows(tokens, depth)
    asked = jnp.pad(asked.astype(F32)[None, :], ((0, 0), (0, depth - asked.shape[0])))

    def whole(shape):
        return pl.BlockSpec(shape, lambda i: (0, 0))

    return pl.pallas_call(
        norm_kernel,
        grid=(tokens // tile,),
        in_specs=[
            pl.BlockSpec((tile, width), lambda i: (i, 0)),
            whole((1, width)),
            whole((16, width)),
            whole(rewards.shape),
            whole(ends.shape),
            whole((segs, 1)),
            whole((1, depth)),
            whole(low.shape),
        ],
        out_specs=[pl.BlockSpec((tile, width), lambda i: (i, 0)), whole((high, depth))],
        out_shape=[
            jax.ShapeDtypeStruct((tokens, width), BF16),
            jax.ShapeDtypeStruct((high, depth), BF16),
        ],
        scratch_shapes=[pltpu.VMEM((16, tokens), F32)],
        compiler_params=ROOM,
        cost_estimate=pl.CostEstimate(
            flops=10 * tokens * width, bytes_accessed=4 * tokens * width, transcendentals=0
        ),
        name="normalize",
    )(
        rows,
        norm_gain.reshape(1, width),
        jnp.broadcast_to(value_weight[None, :], (16, width)),
        rewards,
        ends,
        tails.reshape(segs, 1),
        asked,
        low,
    )


def weight_kernel(plan, segs, samples, total, here_ref, *refs):
    pieces, (weight_ref, mass_ref, norm_ref, known_ref) = refs[: 2 * plan.Y], refs[2 * plan.Y :]
    lanes = weight_ref.shape[1]
    steps = lanes // segs
    owners = plan.C * plan.Y
    c = here_ref[1]
    me = here_ref[0] * plan.C + c
    depth = pieces[0].shape[-1]
    parts = lanes // depth
    for other in range(2):
        for dy in range(plan.Y):
            for dx in range(plan.X):
                for dz in range(plan.Z):
                    row = (other * plan.Y + dy) * plan.mp + dx * plan.Z + dz
                    sent = pieces[other * plan.Y + dy][dx, dz, plan.block :, :].astype(F32)
                    if plan.swap and dy != dx:
                        turned = pieces[other * plan.Y + dx][dy, dz, plan.block :, :].astype(F32)
                        sent = jnp.where(c == other, sent, turned)
                    value = (sent[:parts] + sent[parts : 2 * parts]) + sent[2 * parts : 3 * parts]
                    for i in range(parts):
                        known_ref[row : row + 1, i * depth : (i + 1) * depth] = value[i : i + 1]
                    known_ref[row : row + 1, lanes : lanes + depth] = sent[3 * parts : 3 * parts + 1]
    asked = known_ref[:, lanes:].astype(jnp.int32)
    owner = (asked // segs) ^ me
    slot = ((owner % plan.C) * plan.Y + owner // plan.C) * segs + asked % segs
    code = lax.broadcasted_iota(jnp.int32, (plan.mp, owners * segs), 1)
    times = jnp.zeros((plan.mp, owners * segs), F32)
    for b in range(owners):
        for i in range(samples):
            wanted = slot[b * plan.mp : (b + 1) * plan.mp, i : i + 1]
            times = times + jnp.where(code == wanted, 1.0, 0.0)
    times = times.astype(BF16)
    row = lax.broadcasted_iota(jnp.int32, (owners * segs, lanes), 0)
    lane = lax.broadcasted_iota(jnp.int32, (owners * segs, lanes), 1)
    spread_times = []
    for o in range(owners):
        pick = (row == o * segs + lane // steps).astype(F32).astype(BF16)
        spread_times.append(jnp.dot(times, pick, preferred_element_type=F32))
    times = jnp.concatenate(spread_times, axis=0)
    advantage = known_ref[:, :lanes]
    centered = advantage - jnp.sum(times * advantage) / total
    spread = jnp.sum(times * centered * centered) / total
    normalized = centered * lax.rsqrt(spread + 1e-05)
    weights = times * jnp.exp(jnp.minimum(normalized, 3.0))
    weight_ref[...] = weights[0:1, :]
    mass_ref[0, 0] = jnp.sum(weights)
    for o in range(owners):
        norm_ref[o : o + 1, :] = normalized[o * plan.mp : o * plan.mp + 1, :]


def step_weights(plan, here, pieces, segs, samples, lanes, total):
    owners = plan.C * plan.Y
    depth = pieces[0].shape[-1]
    return pl.pallas_call(
        functools.partial(weight_kernel, plan, segs, samples, total),
        in_specs=[SMEM] + [VMEM] * len(pieces),
        out_specs=[VMEM, SMEM, VMEM],
        out_shape=[
            jax.ShapeDtypeStruct((1, lanes), F32),
            jax.ShapeDtypeStruct((1, 1), F32),
            jax.ShapeDtypeStruct((owners, lanes), F32),
        ],
        scratch_shapes=[pltpu.VMEM((owners * plan.mp, lanes + depth), F32)],
        compiler_params=ROOM,
        name="weights",
    )(here, *pieces)


def gradient_chunk(plan, here, sig_ref, n_ref, keep_ref, send_ref):
    y, c, z, x = here
    rows = plan.Y * plan.block
    depth = keep_ref.shape[-1]
    span = plan.X * depth

    def step(plane, carry):
        part = jnp.dot(
            sig_ref[: 2 * rows, :],
            n_ref[:, pl.ds(pl.multiple_of(plane * span, span), span)],
            preferred_element_type=F32,
        )
        keep = jnp.where(c == 0, part[:rows], part[rows:])
        send = jnp.where(c == 0, part[rows:], part[:rows]).astype(BF16)
        dz = plane ^ z
        for line in range(plan.X):
            for col in range(plan.Y):
                where = (slice(col * plan.block, (col + 1) * plan.block), slice(line * depth, (line + 1) * depth))
                p, q = plan.relative(c, y ^ col, x ^ line)
                keep_ref[p, q, dz] = keep[where]
                p, q = plan.relative(1 - c, y ^ col, x ^ line)
                send_ref[p, q, dz] = send[where]
        return carry

    lax.fori_loop(0, plan.Z, step, 0)


def fetch_policy(plan, here, j, pieces, wt_ref, sems):
    y, c, z, x = here
    block = plan.block
    depth = pieces[0].shape[-1]
    copies = []
    for other in range(2):
        core = c ^ other
        for p in range(plan.Y):
            piece = pieces[other * plan.Y + p]
            for q in range(plan.X):
                a, b = plan.relative(core, p, q)
                for dz in range(plan.Z):
                    row = (core * plan.Y + (y ^ a)) * block
                    col = ((z ^ dz) * plan.X + (x ^ b)) * depth
                    copy = pltpu.make_async_copy(
                        piece.at[q, dz, 0:block],
                        wt_ref.at[
                            pl.ds(pl.multiple_of(row, block), block),
                            pl.ds(pl.multiple_of(col, depth), depth),
                        ],
                        sems.at[len(copies)],
                    )
                    copy.start()
                    copies.append(copy)
    return copies


TILE = 256


def chunk_logits(wt_ref, n_ref, l_ref, first_row, top_ref):
    rows = wt_ref.shape[0]

    def step(t, carry):
        part = lax.dot_general(
            wt_ref[...],
            n_ref[pl.ds(pl.multiple_of(t * TILE, TILE), TILE), :],
            (((1,), (1,)), ((), ())),
            preferred_element_type=F32,
        )
        l_ref[t, first_row : first_row + rows, :] = part
        top_ref[t] = jnp.max(part, axis=0, keepdims=True)
        return carry

    lax.fori_loop(0, l_ref.shape[0], step, 0)


def logits_kernel(plan, here_ref, *refs):
    pieces, refs = refs[: 2 * plan.Y], refs[2 * plan.Y :]
    n_ref, l_ref, top_ref, wt_ref, w_sems = refs
    here = tuple(here_ref[i] for i in range(4))
    for copy in fetch_policy(plan, here, 0, pieces, wt_ref, w_sems):
        copy.wait()
    chunk_logits(wt_ref, n_ref, l_ref, 0, top_ref)


def signals(known, l_ref, sig_refs, w_ref, act_ref, top_ref):
    group = 64
    tiles, actions, _ = l_ref.shape
    rows = sig_refs[0].shape[0]

    def step(t, carry):
        top = top_ref[t]
        for j in range(len(known) // 2):
            top = jnp.maximum(top, known[2 * j + 1][t])
        where = pl.ds(pl.multiple_of(t * TILE, TILE), TILE)
        mass = jnp.zeros((8, TILE), F32)
        for a in range(0, actions, group):
            j, first = a // rows, a % rows
            source = known[2 * j][t, first : first + group, :] if 2 * j < len(known) else l_ref[t, a : a + group, :]
            part = jnp.exp(source - top)
            l_ref[t, a : a + group, :] = part
            mass = mass + jnp.sum(part.reshape(group // 8, 8, TILE), axis=0)
        mass = jnp.sum(mass, axis=0, keepdims=True)
        weight = w_ref[:, where]
        chosen = act_ref[:, where]
        scale = weight / mass
        for a in range(0, actions, group):
            row = lax.broadcasted_iota(jnp.int32, (group, TILE), 0) + a
            part = l_ref[t, a : a + group, :] * scale
            part = part - jnp.where(row == chosen, weight, 0.0)
            sig_refs[a // rows][a % rows : a % rows + group, where] = part.astype(BF16)
        return carry

    lax.fori_loop(0, tiles, step, 0)


def signal_kernel(plan, here_ref, w_ref, act_ref, *refs):
    pieces, refs = refs[: 2 * plan.Y], refs[2 * plan.Y :]
    n_ref, refs = refs[0], refs[1:]
    early = plan.J - 1
    known, refs = refs[: 2 * early], refs[2 * early :]
    rest, refs = refs[:early], refs[early:]
    keep_ref, send_ref, wt_ref, l_ref, top_ref, sig_ref, w_sems = refs
    here = tuple(here_ref[i] for i in range(4))
    for copy in fetch_policy(plan, here, early, pieces, wt_ref, w_sems):
        copy.wait()
    chunk_logits(wt_ref, n_ref, l_ref, early * wt_ref.shape[0], top_ref)
    signals(known, l_ref, (sig_ref,) + tuple(rest), w_ref, act_ref, top_ref)
    gradient_chunk(plan, here, sig_ref, n_ref, keep_ref, send_ref)


def gradient_kernel(plan, here_ref, sig_ref, n_ref, keep_ref, send_ref):
    here = tuple(here_ref[i] for i in range(4))
    gradient_chunk(plan, here, sig_ref, n_ref, keep_ref, send_ref)


def chunk_shapes(plan, depth):
    shape = (plan.Y, plan.X, plan.Z, plan.block, depth)
    return [jax.ShapeDtypeStruct(shape, F32), jax.ShapeDtypeStruct(shape, BF16)]


def early_logits(plan, here, pieces, normed, count):
    tokens, width = normed.shape
    rows = count // plan.J
    return pl.pallas_call(
        functools.partial(logits_kernel, plan),
        in_specs=[SMEM] + [VMEM] * (len(pieces) + 1),
        out_specs=[VMEM, VMEM],
        out_shape=[
            jax.ShapeDtypeStruct((tokens // TILE, rows, TILE), F32),
            jax.ShapeDtypeStruct((tokens // TILE, 1, TILE), F32),
        ],
        scratch_shapes=[
            pltpu.VMEM((rows, width), BF16),
            pltpu.SemaphoreType.DMA((len(pieces) * plan.X * plan.Z,)),
        ],
        compiler_params=ROOM,
        cost_estimate=pl.CostEstimate(
            flops=2 * tokens * width * rows,
            bytes_accessed=2 * tokens * width + 2 * width * rows + 4 * tokens * rows,
            transcendentals=0,
        ),
        name="logits",
    )(here, *pieces, normed)


def signal_and_gradient(plan, here, weights, actions, pieces, normed, count):
    tokens, width = normed.shape
    depth = width // plan.mp
    rows = count // plan.J
    known = []
    for piece in pieces[:-1]:
        known += early_logits(plan, here, piece, normed, count)
    last = pieces[-1]
    signal = jax.ShapeDtypeStruct((rows, tokens), BF16)
    *rest, keep, send = pl.pallas_call(
        functools.partial(signal_kernel, plan),
        in_specs=[SMEM, VMEM, VMEM] + [VMEM] * (len(last) + 1 + len(known)),
        out_specs=[VMEM] * (plan.J + 1),
        out_shape=[signal] * (plan.J - 1) + chunk_shapes(plan, depth),
        scratch_shapes=[
            pltpu.VMEM((rows, width), BF16),
            pltpu.VMEM((tokens // TILE, count, TILE), F32),
            pltpu.VMEM((tokens // TILE, 1, TILE), F32),
            pltpu.VMEM((rows, tokens), BF16),
            pltpu.SemaphoreType.DMA((len(last) * plan.X * plan.Z,)),
        ],
        compiler_params=ROOM,
        cost_estimate=pl.CostEstimate(
            flops=4 * tokens * width * rows,
            bytes_accessed=2 * tokens * width + 2 * width * count + 6 * tokens * count,
            transcendentals=tokens * count,
        ),
        name="signal",
    )(here, weights, actions, *last, normed, *known)
    chunks = [(keep, send)]
    for later in rest:
        chunks.append(
            pl.pallas_call(
                functools.partial(gradient_kernel, plan),
                in_specs=[SMEM, VMEM, VMEM],
                out_specs=[VMEM] * 2,
                out_shape=chunk_shapes(plan, depth),
                compiler_params=ROOM,
                cost_estimate=pl.CostEstimate(
                    flops=2 * tokens * width * rows,
                    bytes_accessed=2 * tokens * width + 2 * tokens * count,
                    transcendentals=0,
                ),
                name="gradient",
            )(here, later, normed)
        )
    return chunks


def assemble_kernel(plan, j, here_ref, *refs):
    count = 2 * plan.Y
    pieces, refs = refs[:count], refs[count:]
    near, far = refs[:2]
    actor_ref, update_ref, sems = refs[-3:]
    y, c, z, x = (here_ref[i] for i in range(4))
    depth = near.shape[-2]
    block = plan.block
    copies = []

    def copy(source, target):
        moved = pltpu.make_async_copy(source, target, sems.at[len(copies)])
        moved.start()
        copies.append(moved)

    for other in range(2):
        core = c ^ other
        for dy in range(plan.Y):
            col = ((j * 2 + core) * plan.Y + (y ^ dy)) * block
            copy(
                (far if other else near).at[dy],
                update_ref.at[:, pl.ds(pl.multiple_of(col, block), block)],
            )
        for p in range(plan.Y):
            piece = pieces[other * plan.Y + p]
            for q in range(plan.X):
                a, b = plan.relative(core, p, q)
                for dz in range(plan.Z):
                    col = ((j * 2 + core) * plan.Y + (y ^ a)) * block
                    row = ((z ^ dz) * plan.X + (x ^ b)) * depth
                    copy(
                        piece.at[q, dz],
                        actor_ref.at[
                            pl.ds(pl.multiple_of(row, depth), depth),
                            pl.ds(pl.multiple_of(col, block), block),
                        ],
                    )
    for moved in copies:
        moved.wait()


def assemble(plan, j, here, pieces, near, far, before, width, count):
    depth = width // plan.mp
    taken = len(pieces) + 3
    return pl.pallas_call(
        functools.partial(assemble_kernel, plan, j),
        in_specs=[SMEM] + [VMEM] * (len(pieces) + 2) + [ANY] * len(before),
        out_specs=[ANY] * 2,
        out_shape=[
            jax.ShapeDtypeStruct((width, count), BF16),
            jax.ShapeDtypeStruct((depth, count), F32),
        ],
        scratch_shapes=[
            pltpu.SemaphoreType.DMA((len(pieces) * plan.X * plan.Z + 2 * plan.Y,)),
        ],
        input_output_aliases={taken + i: i for i in range(len(before))},
        compiler_params=pltpu.CompilerParams(vmem_limit_bytes=32 * 2**20),
        name="assemble",
    )(here, *pieces, near, far, *before)


def body(
    features,
    rewards,
    tail_value,
    actions,
    episode_ends,
    sample_owner,
    sample_row,
    norm_gain,
    value_weight,
    policy_weight,
    first_moment,
    second_moment,
):
    owners_all, columns = lax.axis_size("replay"), lax.axis_size("mp")
    segs, seg_len, width = features.shape
    depth, count = policy_weight.shape
    samples = sample_row.shape[0]
    plan = Plan(owners_all, columns, count)
    here = plan.here()
    place = (here[1] * plan.Y + here[0]).reshape(1)
    replay = lax.axis_index("replay")

    low = own_shard(plan, place, policy_weight)
    stages = [plan.gather_column(block) for block in low[:-1]]
    if stages:
        norm_gain = lax.optimization_barrier((norm_gain, stages[0][1]))[0]

    asked = sample_owner[:, 0] * segs + sample_row
    normed, block = normalize(
        features.reshape(segs * seg_len, width),
        norm_gain,
        value_weight,
        rewards,
        episode_ends,
        tail_value,
        asked,
        low[-1],
    )
    stages.append(plan.gather_column(block))
    pieces = [plan.gather_rest(column) for column in stages]
    token_total = owners_all * columns * samples * seg_len
    weights, total_weight, column = step_weights(plan, here, pieces[-1], segs, samples, segs * seg_len, token_total)
    owner = (asked // segs) ^ replay
    slot = ((owner % plan.C) * plan.Y + owner // plan.C) * segs + asked % segs
    local_norm = column.reshape(owners_all * segs, seg_len)[slot].reshape(-1)

    chunks = signal_and_gradient(plan, here, weights, actions.reshape(1, -1), pieces, normed, count)
    outs, terms = (), None
    for j, (keep, send) in enumerate(chunks):
        base, low = plan.reduce(keep, send)
        if terms is not None:
            low, terms = lax.optimization_barrier((low, terms))
        terms = plan.reduce_column(low)
        update, low = own_update(
            plan, j, place, total_weight, base, terms, policy_weight, first_moment, second_moment
        )
        near = jnp.stack([update] + [plan.permute(update, "y", k) for k in range(1, plan.Y)])
        column, near = lax.optimization_barrier((plan.gather_column(low), near))
        far = plan.permute(near, "c", 1)
        outs = assemble(plan, j, here, plan.gather_rest(column), near, far, outs, width, count)
    actor_policy, update = outs
    return (local_norm, update, actor_policy)


def solution(mesh):
    return jax.shard_map(
        body,
        mesh=mesh,
        in_specs=(
            P(ALL, None, None),
            P(ALL, None),
            P(ALL),
            P(ALL, None),
            P(ALL, None),
            P(ALL, None),
            P(ALL),
            P(),
            P(),
            P("mp", None),
            P("mp", None),
            P("mp", None),
        ),
        out_specs=(P(ALL), P("mp", None), P()),
        check_vma=False,
    )
```

```python
import functools

import jax
import jax.numpy as jnp
from jax import lax
from jax.experimental import pallas as pl
from jax.experimental.pallas import tpu as pltpu
from jax.sharding import PartitionSpec as P

DISCOUNT = 0.97
STEP_RATE = 0.002
ALL = ("replay", "mp")
LANES = 128
BF16 = jnp.bfloat16
F32 = jnp.float32
VMEM = pl.BlockSpec(memory_space=pltpu.VMEM)
SMEM = pl.BlockSpec(memory_space=pltpu.SMEM)
ANY = pl.BlockSpec(memory_space=pl.ANY)
HBM = pl.BlockSpec(memory_space=pltpu.HBM)
ROOM = pltpu.CompilerParams(vmem_limit_bytes=32 * 2**20)


def after(value, *others):
    return lax.optimization_barrier((value, others))[0]


class Plan:
    def __init__(self, replay, mp, actions):
        self.C = 2
        self.Y = replay // self.C
        self.Z = 4
        self.X = mp // self.Z
        self.mp = mp
        self.swap = self.X == self.Y
        self.block = LANES
        self.J = max(1, actions // (self.C * self.Y * self.block))

    def permute(self, value, axis, k):
        pairs = []
        for y in range(self.Y):
            for c in range(self.C):
                for z in range(self.Z):
                    for x in range(self.X):
                        along = axis
                        if axis in ("p", "q"):
                            along = "y" if (axis == "p") == (c == 0 or not self.swap) else "x"
                        to = dict(y=y, c=c, z=z, x=x)
                        to[along] ^= k
                        pairs.append((self.index(y, c, z, x), self.index(**to)))
        return lax.ppermute(value, ALL, pairs)

    def index(self, y, c, z, x):
        return (y * self.C + c) * self.mp + z * self.X + x

    def here(self):
        replay, mp = lax.axis_index("replay"), lax.axis_index("mp")
        return jnp.stack([replay // self.C, replay % self.C, mp // self.X, mp % self.X]).astype(jnp.int32)

    def relative(self, core, dy, dx):
        if not self.swap:
            return dy, dx
        return jnp.where(core == 0, dy, dx), jnp.where(core == 0, dx, dy)

    def gather_column(self, block):
        return [block] + [self.permute(block, "z", k) for k in range(1, self.Z)]

    def gather_plane(self, column):
        column = jnp.stack(column)
        return jnp.stack([column] + [self.permute(column, "q", k) for k in range(1, self.X)])

    def gather_near(self, plane):
        return [plane] + [self.permute(plane, "p", k) for k in range(1, self.Y)]

    def gather_far(self, mine):
        return mine + [self.permute(piece, "c", 1) for piece in mine]

    def reduce(self, keep, send):
        total = keep + self.permute(send, "c", 1).astype(F32)
        for axis in ("p", "q"):
            low = total[1:].astype(BF16)
            total = total[0]
            for k in range(1, low.shape[0] + 1):
                total = total + self.permute(low[k - 1], axis, k).astype(F32)
        return total, [total[k].astype(BF16) for k in range(1, self.Z)]

    def reduce_column(self, low):
        return [self.permute(low[k - 1], "z", k) for k in range(1, self.Z)]


def shard_kernel(plan, place_ref, w_hbm, *refs):
    outs, stage, sems = refs[: plan.J], refs[plan.J], refs[plan.J + 1]
    block = plan.block
    copies = []
    for j in range(plan.J):
        start = pl.multiple_of((j * 2 * plan.Y + place_ref[0]) * block, block)
        copy = pltpu.make_async_copy(w_hbm.at[:, pl.ds(start, block)], stage.at[j], sems.at[j])
        copy.start()
        copies.append(copy)
    for j in range(plan.J):
        copies[j].wait()
        outs[j][...] = stage[j].T.astype(BF16)


def own_shard(plan, place, policy_weight):
    depth = policy_weight.shape[0]
    block = plan.block
    return pl.pallas_call(
        functools.partial(shard_kernel, plan),
        in_specs=[SMEM, ANY],
        out_specs=[VMEM] * plan.J,
        out_shape=[jax.ShapeDtypeStruct((block, depth), BF16)] * plan.J,
        scratch_shapes=[pltpu.VMEM((plan.J, depth, block), F32), pltpu.SemaphoreType.DMA((plan.J,))],
        name="shard",
    )(place, policy_weight)


def update_kernel(count, block, first, place_ref, mass_ref, base_ref, *refs):
    terms, (w_ref, m_ref, v_ref, update_ref, low_ref) = refs[:count], refs[count:]
    own = (slice(None), pl.ds(pl.multiple_of((first + place_ref[0]) * block, block), block))
    total = base_ref[0]
    for term in terms:
        total = total + term[...].astype(F32)
    gradient = total.T / mass_ref[0, 0]
    first_new = 0.9 * m_ref[own] + 0.1 * gradient
    second_new = 0.95 * v_ref[own] + 0.05 * gradient * gradient
    update = first_new / (jnp.sqrt(second_new) + 1e-08)
    update_ref[...] = update
    low_ref[...] = (w_ref[own] - STEP_RATE * update).astype(BF16)


def own_update(plan, j, place, mass, base, terms, policy_weight, first_moment, second_moment):
    depth = policy_weight.shape[0]
    block = plan.block
    return pl.pallas_call(
        functools.partial(update_kernel, len(terms), block, j * 2 * plan.Y),
        in_specs=[SMEM, SMEM] + [VMEM] * (len(terms) + 4),
        out_specs=[VMEM, VMEM],
        out_shape=[
            jax.ShapeDtypeStruct((depth, block), F32),
            jax.ShapeDtypeStruct((depth, block), BF16),
        ],
        compiler_params=pltpu.CompilerParams(vmem_limit_bytes=16 * 2**20),
        name="update",
    )(place, mass, base, *terms, policy_weight, first_moment, second_moment)


def spread_rows(rows, lanes):
    n, steps = rows.shape
    lane = lax.broadcasted_iota(jnp.int32, (steps, lanes), 1)
    pick = (lane % steps == lax.broadcasted_iota(jnp.int32, (steps, lanes), 0)).astype(F32).astype(BF16)
    wide = jnp.dot(rows.astype(BF16), pick, preferred_element_type=F32)
    lane = lax.broadcasted_iota(jnp.int32, (n, lanes), 1)
    own = lane // steps == lax.broadcasted_iota(jnp.int32, (n, lanes), 0)
    return jnp.sum(jnp.where(own, wide, 0.0), axis=0, keepdims=True)


def norm_kernel(x_ref, gain_ref, value_ref, r_ref, e_ref, tail_ref, ask_ref, low_ref, out_ref, block_ref, val_ref):
    wide = x_ref[...].astype(F32)
    mean_square = jnp.mean(wide * wide, axis=-1, keepdims=True)
    normed = (wide * lax.rsqrt(mean_square + 1e-05) * gain_ref[...]).astype(BF16)
    out_ref[...] = normed
    tile = normed.shape[0]
    step = pl.program_id(0)
    val_ref[:, pl.ds(pl.multiple_of(step * tile, tile), tile)] = lax.dot_general(
        value_ref[...], normed, (((1,), (1,)), ((), ())), preferred_element_type=F32
    )

    @pl.when(step == pl.num_programs(0) - 1)
    def _():
        segs, seg_len = r_ref.shape
        lanes = segs * seg_len
        lane = lax.broadcasted_iota(jnp.int32, (1, lanes), 1)
        last = lane % seg_len == seg_len - 1
        ends = spread_rows(e_ref[...].astype(F32), lanes)
        tails = spread_rows(jnp.broadcast_to(tail_ref[...].astype(F32), (segs, seg_len)), lanes)
        decay = DISCOUNT * (1.0 - ends)
        total = spread_rows(r_ref[...], lanes) + jnp.where(last, decay * tails, 0.0)
        decay = jnp.where(last, 0.0, decay)
        reach = 1
        while reach < seg_len:
            total = total + decay * pltpu.roll(total, lanes - reach, axis=1)
            decay = decay * pltpu.roll(decay, lanes - reach, axis=1)
            reach *= 2
        rest = total - val_ref[0:1, :]
        block, depth = low_ref.shape
        rows = []
        for _ in range(3):
            term = rest.astype(BF16).astype(F32)
            rest = rest - term
            rows += [term[:, i : i + depth] for i in range(0, lanes, depth)]
        rows.append(ask_ref[...])
        rows.append(jnp.zeros((block_ref.shape[0] - block - len(rows), depth), F32))
        block_ref[:block, :] = low_ref[...]
        block_ref[block:, :] = jnp.concatenate(rows, axis=0).astype(BF16)


def payload_rows(lanes, depth):
    return -(-(3 * lanes // depth + 1) // 16) * 16


def normalize(rows, norm_gain, value_weight, rewards, ends, tails, asked, low):
    tokens, width = rows.shape
    tile = 256
    block, depth = low.shape
    segs = tails.shape[0]
    high = block + payload_rows(tokens, depth)
    asked = jnp.pad(asked.astype(F32)[None, :], ((0, 0), (0, depth - asked.shape[0])))

    def whole(shape):
        return pl.BlockSpec(shape, lambda i: (0, 0))

    return pl.pallas_call(
        norm_kernel,
        grid=(tokens // tile,),
        in_specs=[
            pl.BlockSpec((tile, width), lambda i: (i, 0)),
            whole((1, width)),
            whole((16, width)),
            whole(rewards.shape),
            whole(ends.shape),
            whole((segs, 1)),
            whole((1, depth)),
            whole(low.shape),
        ],
        out_specs=[pl.BlockSpec((tile, width), lambda i: (i, 0)), whole((high, depth))],
        out_shape=[
            jax.ShapeDtypeStruct((tokens, width), BF16),
            jax.ShapeDtypeStruct((high, depth), BF16),
        ],
        scratch_shapes=[pltpu.VMEM((16, tokens), F32)],
        compiler_params=ROOM,
        cost_estimate=pl.CostEstimate(
            flops=10 * tokens * width, bytes_accessed=4 * tokens * width, transcendentals=0
        ),
        name="normalize",
    )(
        rows,
        norm_gain.reshape(1, width),
        jnp.broadcast_to(value_weight[None, :], (16, width)),
        rewards,
        ends,
        tails.reshape(segs, 1),
        asked,
        low,
    )


def step_weights(plan, here, segs, samples, total, pieces, weight_ref, mass_ref, norm_ref, known_ref):
    lanes = weight_ref.shape[1]
    steps = lanes // segs
    owners = plan.C * plan.Y
    c = here[1]
    me = here[0] * plan.C + c
    depth = pieces[0].shape[-1]
    parts = lanes // depth
    for other in range(2):
        for dy in range(plan.Y):
            for dx in range(plan.X):
                for dz in range(plan.Z):
                    row = (other * plan.Y + dy) * plan.mp + dx * plan.Z + dz
                    sent = pieces[other * plan.Y + dy][dx, dz, plan.block :, :].astype(F32)
                    if plan.swap and dy != dx:
                        turned = pieces[other * plan.Y + dx][dy, dz, plan.block :, :].astype(F32)
                        sent = jnp.where(c == other, sent, turned)
                    value = (sent[:parts] + sent[parts : 2 * parts]) + sent[2 * parts : 3 * parts]
                    for i in range(parts):
                        known_ref[row : row + 1, i * depth : (i + 1) * depth] = value[i : i + 1]
                    known_ref[row : row + 1, lanes : lanes + depth] = sent[3 * parts : 3 * parts + 1]
    asked = known_ref[:, lanes:].astype(jnp.int32)
    owner = (asked // segs) ^ me
    slot = ((owner % plan.C) * plan.Y + owner // plan.C) * segs + asked % segs
    code = lax.broadcasted_iota(jnp.int32, (plan.mp, owners * segs), 1)
    times = jnp.zeros((plan.mp, owners * segs), F32)
    for b in range(owners):
        for i in range(samples):
            wanted = slot[b * plan.mp : (b + 1) * plan.mp, i : i + 1]
            times = times + jnp.where(code == wanted, 1.0, 0.0)
    times = times.astype(BF16)
    row = lax.broadcasted_iota(jnp.int32, (owners * segs, lanes), 0)
    lane = lax.broadcasted_iota(jnp.int32, (owners * segs, lanes), 1)
    spread_times = []
    for o in range(owners):
        pick = (row == o * segs + lane // steps).astype(F32).astype(BF16)
        spread_times.append(jnp.dot(times, pick, preferred_element_type=F32))
    times = jnp.concatenate(spread_times, axis=0)
    advantage = known_ref[:, :lanes]
    centered = advantage - jnp.sum(times * advantage) / total
    spread = jnp.sum(times * centered * centered) / total
    normalized = centered * lax.rsqrt(spread + 1e-05)
    weights = times * jnp.exp(jnp.minimum(normalized, 3.0))
    weight_ref[...] = weights[0:1, :]
    mass_ref[0, 0] = jnp.sum(weights)
    for o in range(owners):
        norm_ref[o : o + 1, :] = normalized[o * plan.mp : o * plan.mp + 1, :]


def gradient_chunk(plan, here, sig_ref, n_ref, keep_ref, send_ref):
    y, c, z, x = here
    rows = plan.Y * plan.block
    depth = keep_ref.shape[-1]
    span = plan.X * depth

    def step(plane, carry):
        part = jnp.dot(
            sig_ref[: 2 * rows, :],
            n_ref[:, pl.ds(pl.multiple_of(plane * span, span), span)],
            preferred_element_type=F32,
        )
        keep = jnp.where(c == 0, part[:rows], part[rows:])
        send = jnp.where(c == 0, part[rows:], part[:rows]).astype(BF16)
        dz = plane ^ z
        for line in range(plan.X):
            for col in range(plan.Y):
                where = (slice(col * plan.block, (col + 1) * plan.block), slice(line * depth, (line + 1) * depth))
                p, q = plan.relative(c, y ^ col, x ^ line)
                keep_ref[p, q, dz] = keep[where]
                p, q = plan.relative(1 - c, y ^ col, x ^ line)
                send_ref[p, q, dz] = send[where]
        return carry

    lax.fori_loop(0, plan.Z, step, 0)


def fetch_policy(plan, here, j, pieces, wt_ref, sems):
    y, c, z, x = here
    block = plan.block
    depth = pieces[0].shape[-1]
    copies = []
    for other in range(2):
        core = c ^ other
        for p in range(plan.Y):
            piece = pieces[other * plan.Y + p]
            for q in range(plan.X):
                a, b = plan.relative(core, p, q)
                for dz in range(plan.Z):
                    row = (core * plan.Y + (y ^ a)) * block
                    col = ((z ^ dz) * plan.X + (x ^ b)) * depth
                    copy = pltpu.make_async_copy(
                        piece.at[q, dz, 0:block],
                        wt_ref.at[
                            pl.ds(pl.multiple_of(row, block), block),
                            pl.ds(pl.multiple_of(col, depth), depth),
                        ],
                        sems.at[len(copies)],
                    )
                    copy.start()
                    copies.append(copy)
    return copies


TILE = 256


def chunk_logits(wt_ref, n_ref, l_ref, first_row, top_ref):
    rows = wt_ref.shape[0]

    def step(t, carry):
        part = lax.dot_general(
            wt_ref[...],
            n_ref[pl.ds(pl.multiple_of(t * TILE, TILE), TILE), :],
            (((1,), (1,)), ((), ())),
            preferred_element_type=F32,
        )
        l_ref[t, first_row : first_row + rows, :] = part
        top_ref[t] = jnp.max(part, axis=0, keepdims=True)
        return carry

    lax.fori_loop(0, l_ref.shape[0], step, 0)


def logits_kernel(plan, here_ref, *refs):
    pieces, refs = refs[: 2 * plan.Y], refs[2 * plan.Y :]
    n_ref, l_ref, top_ref, wt_ref, w_sems = refs
    here = tuple(here_ref[i] for i in range(4))
    copies = fetch_policy(plan, here, 0, pieces, wt_ref, w_sems)
    for copy in copies:
        copy.wait()
    chunk_logits(wt_ref, n_ref, l_ref, 0, top_ref)


def signals(known, l_ref, sig_refs, w_ref, act_ref, top_ref):
    group = 64
    tiles, actions, _ = l_ref.shape
    rows = sig_refs[0].shape[0]

    def step(t, carry):
        top = top_ref[t]
        for j in range(len(known) // 2):
            top = jnp.maximum(top, known[2 * j + 1][t])
        where = pl.ds(pl.multiple_of(t * TILE, TILE), TILE)
        mass = jnp.zeros((8, TILE), F32)
        for a in range(0, actions, group):
            j, first = a // rows, a % rows
            source = known[2 * j][t, first : first + group, :] if 2 * j < len(known) else l_ref[t, a : a + group, :]
            part = jnp.exp(source - top)
            l_ref[t, a : a + group, :] = part
            mass = mass + jnp.sum(part.reshape(group // 8, 8, TILE), axis=0)
        mass = jnp.sum(mass, axis=0, keepdims=True)
        weight = w_ref[:, where]
        chosen = act_ref[:, where]
        scale = weight / mass
        for a in range(0, actions, group):
            row = lax.broadcasted_iota(jnp.int32, (group, TILE), 0) + a
            part = l_ref[t, a : a + group, :] * scale
            part = part - jnp.where(row == chosen, weight, 0.0)
            sig_refs[a // rows][a % rows : a % rows + group, where] = part.astype(BF16)
        return carry

    lax.fori_loop(0, tiles, step, 0)


def signal_kernel(plan, segs, samples, total, here_ref, act_ref, *refs):
    pieces, refs = refs[: 2 * plan.Y], refs[2 * plan.Y :]
    n_ref, refs = refs[0], refs[1:]
    early = plan.J - 1
    known, refs = refs[: 2 * early], refs[2 * early :]
    mass_ref, norm_ref, refs = refs[0], refs[1], refs[2:]
    rest, refs = refs[:early], refs[early:]
    keep_ref, send_ref, wt_ref, w_ref, known_ref, l_ref, top_ref, sig_ref, w_sems = refs
    here = tuple(here_ref[i] for i in range(4))
    copies = fetch_policy(plan, here, early, pieces, wt_ref, w_sems)
    step_weights(plan, here, segs, samples, total, pieces, w_ref, mass_ref, norm_ref, known_ref)
    for copy in copies:
        copy.wait()
    chunk_logits(wt_ref, n_ref, l_ref, early * wt_ref.shape[0], top_ref)
    signals(known, l_ref, (sig_ref,) + tuple(rest), w_ref, act_ref, top_ref)
    gradient_chunk(plan, here, sig_ref, n_ref, keep_ref, send_ref)


def gradient_kernel(plan, here_ref, sig_ref, n_ref, keep_ref, send_ref):
    here = tuple(here_ref[i] for i in range(4))
    gradient_chunk(plan, here, sig_ref, n_ref, keep_ref, send_ref)


def chunk_shapes(plan, depth):
    shape = (plan.Y, plan.X, plan.Z, plan.block, depth)
    return [jax.ShapeDtypeStruct(shape, F32), jax.ShapeDtypeStruct(shape, BF16)]


def early_logits(plan, here, pieces, normed, count):
    tokens, width = normed.shape
    rows = count // plan.J
    return pl.pallas_call(
        functools.partial(logits_kernel, plan),
        in_specs=[SMEM] + [VMEM] * len(pieces) + [VMEM],
        out_specs=[VMEM, VMEM],
        out_shape=[
            jax.ShapeDtypeStruct((tokens // TILE, rows, TILE), F32),
            jax.ShapeDtypeStruct((tokens // TILE, 1, TILE), F32),
        ],
        scratch_shapes=[
            pltpu.VMEM((rows, width), BF16),
            pltpu.SemaphoreType.DMA((len(pieces) * plan.X * plan.Z,)),
        ],
        compiler_params=ROOM,
        cost_estimate=pl.CostEstimate(
            flops=2 * tokens * width * rows,
            bytes_accessed=2 * tokens * width + 2 * width * rows + 4 * tokens * rows,
            transcendentals=0,
        ),
        name="logits",
    )(here, *pieces, normed)


def signal_and_gradient(plan, here, actions, last, normed, known, count, segs, samples, total):
    tokens, width = normed.shape
    depth = width // plan.mp
    rows = count // plan.J
    known = [value for pair in known for value in pair]
    signal = jax.ShapeDtypeStruct((rows, tokens), BF16)
    owners = plan.C * plan.Y
    mass, norm, *rest, keep, send = pl.pallas_call(
        functools.partial(signal_kernel, plan, segs, samples, total),
        in_specs=[SMEM, VMEM] + [VMEM] * len(last) + [VMEM] + [VMEM] * len(known),
        out_specs=[SMEM] + [VMEM] * (plan.J + 2),
        out_shape=[
            jax.ShapeDtypeStruct((1, 1), F32),
            jax.ShapeDtypeStruct((owners, tokens), F32),
        ]
        + [signal] * (plan.J - 1)
        + chunk_shapes(plan, depth),
        scratch_shapes=[
            pltpu.VMEM((rows, width), BF16),
            pltpu.VMEM((1, tokens), F32),
            pltpu.VMEM((owners * plan.mp, tokens + depth), F32),
            pltpu.VMEM((tokens // TILE, count, TILE), F32),
            pltpu.VMEM((tokens // TILE, 1, TILE), F32),
            pltpu.VMEM((rows, tokens), BF16),
            pltpu.SemaphoreType.DMA((len(last) * plan.X * plan.Z,)),
        ],
        compiler_params=ROOM,
        cost_estimate=pl.CostEstimate(
            flops=4 * tokens * width * rows,
            bytes_accessed=2 * tokens * width + 2 * width * count + 6 * tokens * count,
            transcendentals=tokens * count,
        ),
        name="signal",
    )(here, actions, *last, normed, *known)
    chunks = [(keep, send)]
    for later in rest:
        chunks.append(
            pl.pallas_call(
                functools.partial(gradient_kernel, plan),
                in_specs=[SMEM, VMEM, VMEM],
                out_specs=[VMEM] * 2,
                out_shape=chunk_shapes(plan, depth),
                compiler_params=ROOM,
                cost_estimate=pl.CostEstimate(
                    flops=2 * tokens * width * rows,
                    bytes_accessed=2 * tokens * width + 2 * tokens * count,
                    transcendentals=0,
                ),
                name="gradient",
            )(here, later, normed)
        )
    return mass, norm, chunks


def assemble_kernel(plan, here_ref, *refs):
    count = 2 * plan.Y * plan.J
    pieces, updates = refs[:count], refs[count : count + 2 * plan.J]
    actor_ref, update_ref, sems = refs[-3:]
    y, c, z, x = (here_ref[i] for i in range(4))
    depth = updates[0].shape[-2]
    block = plan.block
    copies = []

    def copy(source, target):
        moved = pltpu.make_async_copy(source, target, sems.at[len(copies)])
        moved.start()
        copies.append(moved)

    for j in range(plan.J):
        for other in range(2):
            core = c ^ other
            for dy in range(plan.Y):
                col = ((j * 2 + core) * plan.Y + (y ^ dy)) * block
                copy(
                    updates[2 * j + other].at[dy],
                    update_ref.at[:, pl.ds(pl.multiple_of(col, block), block)],
                )
            for p in range(plan.Y):
                piece = pieces[(j * 2 + other) * plan.Y + p]
                for q in range(plan.X):
                    a, b = plan.relative(core, p, q)
                    for dz in range(plan.Z):
                        col = ((j * 2 + core) * plan.Y + (y ^ a)) * block
                        row = ((z ^ dz) * plan.X + (x ^ b)) * depth
                        copy(
                            piece.at[q, dz],
                            actor_ref.at[
                                pl.ds(pl.multiple_of(row, depth), depth),
                                pl.ds(pl.multiple_of(col, block), block),
                            ],
                        )
    for moved in copies:
        moved.wait()


def assemble(plan, here, pieces, updates, width, count):
    depth = width // plan.mp
    return pl.pallas_call(
        functools.partial(assemble_kernel, plan),
        in_specs=[SMEM] + [VMEM] * (len(pieces) + len(updates)),
        out_specs=[ANY] * 2,
        out_shape=[
            jax.ShapeDtypeStruct((width, count), BF16),
            jax.ShapeDtypeStruct((depth, count), F32),
        ],
        scratch_shapes=[
            pltpu.SemaphoreType.DMA((len(pieces) * plan.X * plan.Z + len(updates) * plan.Y,)),
        ],
        compiler_params=ROOM,
        name="assemble",
    )(here, *pieces, *updates)


def body(
    features,
    rewards,
    tail_value,
    actions,
    episode_ends,
    sample_owner,
    sample_row,
    norm_gain,
    value_weight,
    policy_weight,
    first_moment,
    second_moment,
):
    owners_all, columns = lax.axis_size("replay"), lax.axis_size("mp")
    segs, seg_len, width = features.shape
    depth, count = policy_weight.shape
    samples = sample_row.shape[0]
    plan = Plan(owners_all, columns, count)
    here = plan.here()
    place = (here[1] * plan.Y + here[0]).reshape(1)
    replay = lax.axis_index("replay")

    low = own_shard(plan, place, policy_weight)
    stages = [plan.gather_column(block) for block in low[:-1]]
    if stages:
        norm_gain = after(norm_gain, stages[0][1])

    asked = sample_owner[:, 0] * segs + sample_row
    normed, block = normalize(
        features.reshape(segs * seg_len, width),
        norm_gain,
        value_weight,
        rewards,
        episode_ends,
        tail_value,
        asked,
        low[-1],
    )
    column = plan.gather_column(block)
    planes = [plan.gather_plane([after(first[0], block)] + first[1:]) for first in stages]
    near = [plan.gather_near(after(plane, column[1])) for plane in planes]
    mine = plan.gather_near(plan.gather_plane(column))
    pieces = [plan.gather_far(piece) for piece in near]
    known = [early_logits(plan, here, piece, normed, count) for piece in pieces]
    pieces.append(plan.gather_far(mine))

    token_total = owners_all * columns * samples * seg_len
    total_weight, column, chunks = signal_and_gradient(
        plan, here, actions.reshape(1, -1), pieces[-1], normed, known, count, segs, samples, token_total
    )
    owner = (asked // segs) ^ replay
    slot = ((owner % plan.C) * plan.Y + owner // plan.C) * segs + asked % segs
    local_norm = column.reshape(owners_all * segs, seg_len)[slot].reshape(-1)
    fresh, updates, terms = [], [], None
    for j, (keep, send) in enumerate(chunks):
        base, low = plan.reduce(keep, send)
        if terms is not None:
            low, terms = lax.optimization_barrier((low, terms))
        terms = plan.reduce_column(low)
        update, low = own_update(
            plan, j, place, total_weight, base, terms, policy_weight, first_moment, second_moment
        )
        near = jnp.stack([update] + [plan.permute(update, "y", k) for k in range(1, plan.Y)])
        column, near = lax.optimization_barrier((plan.gather_column(low), near))
        updates += [near, plan.permute(near, "c", 1)]
        fresh += plan.gather_far(plan.gather_near(plan.gather_plane(column)))
    actor_policy, update = assemble(plan, here, fresh, updates, width, count)
    return (local_norm, update, actor_policy)


def solution(mesh):
    return jax.shard_map(
        body,
        mesh=mesh,
        in_specs=(
            P(ALL, None, None),
            P(ALL, None),
            P(ALL),
            P(ALL, None),
            P(ALL, None),
            P(ALL, None),
            P(ALL),
            P(),
            P(),
            P("mp", None),
            P("mp", None),
            P("mp", None),
        ),
        out_specs=(P(ALL), P("mp", None), P()),
        check_vma=False,
    )
```

```python
import functools

import jax
import jax.numpy as jnp
from jax import lax
from jax.experimental import pallas as pl
from jax.experimental.pallas import tpu as pltpu
from jax.sharding import PartitionSpec as P

DISCOUNT = 0.97
STEP_RATE = 0.002
ALL = ("replay", "mp")
LANES = 128
BF16 = jnp.bfloat16
F32 = jnp.float32
VMEM = pl.BlockSpec(memory_space=pltpu.VMEM)
SMEM = pl.BlockSpec(memory_space=pltpu.SMEM)
ANY = pl.BlockSpec(memory_space=pl.ANY)
HBM = pl.BlockSpec(memory_space=pltpu.HBM)
ROOM = pltpu.CompilerParams(vmem_limit_bytes=32 * 2**20)


def after(value, *others):
    return lax.optimization_barrier((value, others))[0]


class Plan:
    def __init__(self, replay, mp, actions):
        self.C = 2
        self.Y = replay // self.C
        self.Z = 4
        self.X = mp // self.Z
        self.mp = mp
        self.swap = self.X == self.Y
        self.block = LANES
        self.J = max(1, actions // (self.C * self.Y * self.block))

    def permute(self, value, axis, k):
        pairs = []
        for y in range(self.Y):
            for c in range(self.C):
                for z in range(self.Z):
                    for x in range(self.X):
                        along = axis
                        if axis in ("p", "q"):
                            along = "y" if (axis == "p") == (c == 0 or not self.swap) else "x"
                        to = dict(y=y, c=c, z=z, x=x)
                        to[along] ^= k
                        pairs.append((self.index(y, c, z, x), self.index(**to)))
        return lax.ppermute(value, ALL, pairs)

    def index(self, y, c, z, x):
        return (y * self.C + c) * self.mp + z * self.X + x

    def here(self):
        replay, mp = lax.axis_index("replay"), lax.axis_index("mp")
        return jnp.stack([replay // self.C, replay % self.C, mp // self.X, mp % self.X]).astype(jnp.int32)

    def relative(self, core, dy, dx):
        if not self.swap:
            return dy, dx
        return jnp.where(core == 0, dy, dx), jnp.where(core == 0, dx, dy)

    def gather_column(self, block):
        return [block] + [self.permute(block, "z", k) for k in range(1, self.Z)]

    def gather_plane(self, column):
        column = jnp.stack(column)
        return jnp.stack([column] + [self.permute(column, "q", k) for k in range(1, self.X)])

    def gather_near(self, plane):
        return [plane] + [self.permute(plane, "p", k) for k in range(1, self.Y)]

    def gather_far(self, mine):
        return mine + [self.permute(piece, "c", 1) for piece in mine]

    def reduce(self, keep, send):
        total = keep + self.permute(send, "c", 1).astype(F32)
        for axis in ("p", "q"):
            low = total[1:].astype(BF16)
            total = total[0]
            for k in range(1, low.shape[0] + 1):
                total = total + self.permute(low[k - 1], axis, k).astype(F32)
        return total, [total[k].astype(BF16) for k in range(1, self.Z)]

    def reduce_column(self, low):
        return [self.permute(low[k - 1], "z", k) for k in range(1, self.Z)]


def shard_kernel(plan, place_ref, w_hbm, *refs):
    outs, stage, sems = refs[: plan.J], refs[plan.J], refs[plan.J + 1]
    block = plan.block
    copies = []
    for j in range(plan.J):
        start = pl.multiple_of((j * 2 * plan.Y + place_ref[0]) * block, block)
        copy = pltpu.make_async_copy(w_hbm.at[:, pl.ds(start, block)], stage.at[j], sems.at[j])
        copy.start()
        copies.append(copy)
    for j in range(plan.J):
        copies[j].wait()
        outs[j][...] = stage[j].T.astype(BF16)


def own_shard(plan, place, policy_weight):
    depth = policy_weight.shape[0]
    block = plan.block
    return pl.pallas_call(
        functools.partial(shard_kernel, plan),
        in_specs=[SMEM, ANY],
        out_specs=[VMEM] * plan.J,
        out_shape=[jax.ShapeDtypeStruct((block, depth), BF16)] * plan.J,
        scratch_shapes=[pltpu.VMEM((plan.J, depth, block), F32), pltpu.SemaphoreType.DMA((plan.J,))],
        name="shard",
    )(place, policy_weight)


def update_kernel(count, block, first, place_ref, mass_ref, base_ref, *refs):
    terms, (w_ref, m_ref, v_ref, update_ref, low_ref) = refs[:count], refs[count:]
    own = (slice(None), pl.ds(pl.multiple_of((first + place_ref[0]) * block, block), block))
    total = base_ref[0]
    for term in terms:
        total = total + term[...].astype(F32)
    gradient = total.T / mass_ref[0, 0]
    first_new = 0.9 * m_ref[own] + 0.1 * gradient
    second_new = 0.95 * v_ref[own] + 0.05 * gradient * gradient
    update = first_new / (jnp.sqrt(second_new) + 1e-08)
    update_ref[...] = update
    low_ref[...] = (w_ref[own] - STEP_RATE * update).astype(BF16)


def own_update(plan, j, place, mass, base, terms, policy_weight, first_moment, second_moment):
    depth = policy_weight.shape[0]
    block = plan.block
    return pl.pallas_call(
        functools.partial(update_kernel, len(terms), block, j * 2 * plan.Y),
        in_specs=[SMEM, SMEM] + [VMEM] * (len(terms) + 4),
        out_specs=[VMEM, VMEM],
        out_shape=[
            jax.ShapeDtypeStruct((depth, block), F32),
            jax.ShapeDtypeStruct((depth, block), BF16),
        ],
        compiler_params=pltpu.CompilerParams(vmem_limit_bytes=16 * 2**20),
        name="update",
    )(place, mass, base, *terms, policy_weight, first_moment, second_moment)


def spread_rows(rows, lanes):
    n, steps = rows.shape
    lane = lax.broadcasted_iota(jnp.int32, (steps, lanes), 1)
    pick = (lane % steps == lax.broadcasted_iota(jnp.int32, (steps, lanes), 0)).astype(F32).astype(BF16)
    wide = jnp.dot(rows.astype(BF16), pick, preferred_element_type=F32)
    lane = lax.broadcasted_iota(jnp.int32, (n, lanes), 1)
    own = lane // steps == lax.broadcasted_iota(jnp.int32, (n, lanes), 0)
    return jnp.sum(jnp.where(own, wide, 0.0), axis=0, keepdims=True)


def norm_kernel(x_ref, gain_ref, value_ref, r_ref, e_ref, tail_ref, ask_ref, low_ref, out_ref, block_ref, val_ref):
    wide = x_ref[...].astype(F32)
    mean_square = jnp.mean(wide * wide, axis=-1, keepdims=True)
    normed = (wide * lax.rsqrt(mean_square + 1e-05) * gain_ref[...]).astype(BF16)
    out_ref[...] = normed
    tile = normed.shape[0]
    step = pl.program_id(0)
    val_ref[:, pl.ds(pl.multiple_of(step * tile, tile), tile)] = lax.dot_general(
        value_ref[...], normed, (((1,), (1,)), ((), ())), preferred_element_type=F32
    )

    @pl.when(step == pl.num_programs(0) - 1)
    def _():
        segs, seg_len = r_ref.shape
        lanes = segs * seg_len
        lane = lax.broadcasted_iota(jnp.int32, (1, lanes), 1)
        last = lane % seg_len == seg_len - 1
        ends = spread_rows(e_ref[...].astype(F32), lanes)
        tails = spread_rows(jnp.broadcast_to(tail_ref[...].astype(F32), (segs, seg_len)), lanes)
        decay = DISCOUNT * (1.0 - ends)
        total = spread_rows(r_ref[...], lanes) + jnp.where(last, decay * tails, 0.0)
        decay = jnp.where(last, 0.0, decay)
        reach = 1
        while reach < seg_len:
            total = total + decay * pltpu.roll(total, lanes - reach, axis=1)
            decay = decay * pltpu.roll(decay, lanes - reach, axis=1)
            reach *= 2
        rest = total - val_ref[0:1, :]
        block, depth = low_ref.shape
        rows = []
        for _ in range(3):
            term = rest.astype(BF16).astype(F32)
            rest = rest - term
            rows += [term[:, i : i + depth] for i in range(0, lanes, depth)]
        rows.append(ask_ref[...])
        rows.append(jnp.zeros((block_ref.shape[0] - block - len(rows), depth), F32))
        block_ref[:block, :] = low_ref[...]
        block_ref[block:, :] = jnp.concatenate(rows, axis=0).astype(BF16)


def payload_rows(lanes, depth):
    return -(-(3 * lanes // depth + 1) // 16) * 16


def normalize(rows, norm_gain, value_weight, rewards, ends, tails, asked, low):
    tokens, width = rows.shape
    tile = 256
    block, depth = low.shape
    segs = tails.shape[0]
    high = block + payload_rows(tokens, depth)
    asked = jnp.pad(asked.astype(F32)[None, :], ((0, 0), (0, depth - asked.shape[0])))

    def whole(shape):
        return pl.BlockSpec(shape, lambda i: (0, 0))

    return pl.pallas_call(
        norm_kernel,
        grid=(tokens // tile,),
        in_specs=[
            pl.BlockSpec((tile, width), lambda i: (i, 0)),
            whole((1, width)),
            whole((16, width)),
            whole(rewards.shape),
            whole(ends.shape),
            whole((segs, 1)),
            whole((1, depth)),
            whole(low.shape),
        ],
        out_specs=[pl.BlockSpec((tile, width), lambda i: (i, 0)), whole((high, depth))],
        out_shape=[
            jax.ShapeDtypeStruct((tokens, width), BF16),
            jax.ShapeDtypeStruct((high, depth), BF16),
        ],
        scratch_shapes=[pltpu.VMEM((16, tokens), F32)],
        compiler_params=ROOM,
        cost_estimate=pl.CostEstimate(
            flops=10 * tokens * width, bytes_accessed=4 * tokens * width, transcendentals=0
        ),
        name="normalize",
    )(
        rows,
        norm_gain.reshape(1, width),
        jnp.broadcast_to(value_weight[None, :], (16, width)),
        rewards,
        ends,
        tails.reshape(segs, 1),
        asked,
        low,
    )


def step_weights(plan, here, segs, samples, total, pieces, weight_ref, mass_ref, norm_ref, known_ref):
    lanes = weight_ref.shape[1]
    steps = lanes // segs
    owners = plan.C * plan.Y
    c = here[1]
    me = here[0] * plan.C + c
    depth = pieces[0].shape[-1]
    parts = lanes // depth
    for other in range(2):
        for dy in range(plan.Y):
            for dx in range(plan.X):
                for dz in range(plan.Z):
                    row = (other * plan.Y + dy) * plan.mp + dx * plan.Z + dz
                    sent = pieces[other * plan.Y + dy][dx, dz, plan.block :, :].astype(F32)
                    if plan.swap and dy != dx:
                        turned = pieces[other * plan.Y + dx][dy, dz, plan.block :, :].astype(F32)
                        sent = jnp.where(c == other, sent, turned)
                    value = (sent[:parts] + sent[parts : 2 * parts]) + sent[2 * parts : 3 * parts]
                    for i in range(parts):
                        known_ref[row : row + 1, i * depth : (i + 1) * depth] = value[i : i + 1]
                    known_ref[row : row + 1, lanes : lanes + depth] = sent[3 * parts : 3 * parts + 1]
    asked = known_ref[:, lanes:].astype(jnp.int32)
    owner = (asked // segs) ^ me
    slot = ((owner % plan.C) * plan.Y + owner // plan.C) * segs + asked % segs
    code = lax.broadcasted_iota(jnp.int32, (plan.mp, owners * segs), 1)
    times = jnp.zeros((plan.mp, owners * segs), F32)
    for b in range(owners):
        for i in range(samples):
            wanted = slot[b * plan.mp : (b + 1) * plan.mp, i : i + 1]
            times = times + jnp.where(code == wanted, 1.0, 0.0)
    times = times.astype(BF16)
    row = lax.broadcasted_iota(jnp.int32, (owners * segs, lanes), 0)
    lane = lax.broadcasted_iota(jnp.int32, (owners * segs, lanes), 1)
    spread_times = []
    for o in range(owners):
        pick = (row == o * segs + lane // steps).astype(F32).astype(BF16)
        spread_times.append(jnp.dot(times, pick, preferred_element_type=F32))
    times = jnp.concatenate(spread_times, axis=0)
    advantage = known_ref[:, :lanes]
    centered = advantage - jnp.sum(times * advantage) / total
    spread = jnp.sum(times * centered * centered) / total
    normalized = centered * lax.rsqrt(spread + 1e-05)
    weights = times * jnp.exp(jnp.minimum(normalized, 3.0))
    weight_ref[...] = weights[0:1, :]
    mass_ref[0, 0] = jnp.sum(weights)
    for o in range(owners):
        norm_ref[o : o + 1, :] = normalized[o * plan.mp : o * plan.mp + 1, :]


def gradient_chunk(plan, here, sig_ref, n_ref, keep_ref, send_ref):
    y, c, z, x = here
    rows = plan.Y * plan.block
    depth = keep_ref.shape[-1]
    span = plan.X * depth

    def step(plane, carry):
        part = jnp.dot(
            sig_ref[: 2 * rows, :],
            n_ref[:, pl.ds(pl.multiple_of(plane * span, span), span)],
            preferred_element_type=F32,
        )
        keep = jnp.where(c == 0, part[:rows], part[rows:])
        send = jnp.where(c == 0, part[rows:], part[:rows]).astype(BF16)
        dz = plane ^ z
        for line in range(plan.X):
            for col in range(plan.Y):
                where = (slice(col * plan.block, (col + 1) * plan.block), slice(line * depth, (line + 1) * depth))
                p, q = plan.relative(c, y ^ col, x ^ line)
                keep_ref[p, q, dz] = keep[where]
                p, q = plan.relative(1 - c, y ^ col, x ^ line)
                send_ref[p, q, dz] = send[where]
        return carry

    lax.fori_loop(0, plan.Z, step, 0)


def fetch_policy(plan, here, j, pieces, wt_ref, sems):
    y, c, z, x = here
    block = plan.block
    depth = pieces[0].shape[-1]
    copies = []
    for other in range(2):
        core = c ^ other
        for p in range(plan.Y):
            piece = pieces[other * plan.Y + p]
            for q in range(plan.X):
                a, b = plan.relative(core, p, q)
                for dz in range(plan.Z):
                    row = (core * plan.Y + (y ^ a)) * block
                    col = ((z ^ dz) * plan.X + (x ^ b)) * depth
                    copy = pltpu.make_async_copy(
                        piece.at[q, dz, 0:block],
                        wt_ref.at[
                            pl.ds(pl.multiple_of(row, block), block),
                            pl.ds(pl.multiple_of(col, depth), depth),
                        ],
                        sems.at[len(copies)],
                    )
                    copy.start()
                    copies.append(copy)
    return copies


TILE = 256


def chunk_logits(wt_ref, n_ref, l_ref, first_row, top_ref):
    rows = wt_ref.shape[0]

    def step(t, carry):
        part = lax.dot_general(
            wt_ref[...],
            n_ref[pl.ds(pl.multiple_of(t * TILE, TILE), TILE), :],
            (((1,), (1,)), ((), ())),
            preferred_element_type=F32,
        )
        l_ref[t, first_row : first_row + rows, :] = part
        top_ref[t] = jnp.max(part, axis=0, keepdims=True)
        return carry

    lax.fori_loop(0, l_ref.shape[0], step, 0)


def logits_kernel(plan, here_ref, *refs):
    pieces, refs = refs[: 2 * plan.Y], refs[2 * plan.Y :]
    n_ref, l_ref, top_ref, wt_ref, w_sems = refs
    here = tuple(here_ref[i] for i in range(4))
    copies = fetch_policy(plan, here, 0, pieces, wt_ref, w_sems)
    for copy in copies:
        copy.wait()
    chunk_logits(wt_ref, n_ref, l_ref, 0, top_ref)


def signals(known, l_ref, sig_refs, w_ref, act_ref, top_ref):
    group = 64
    tiles, actions, _ = l_ref.shape
    rows = sig_refs[0].shape[0]

    def step(t, carry):
        top = top_ref[t]
        for j in range(len(known) // 2):
            top = jnp.maximum(top, known[2 * j + 1][t])
        where = pl.ds(pl.multiple_of(t * TILE, TILE), TILE)
        mass = jnp.zeros((8, TILE), F32)
        for a in range(0, actions, group):
            j, first = a // rows, a % rows
            source = known[2 * j][t, first : first + group, :] if 2 * j < len(known) else l_ref[t, a : a + group, :]
            part = jnp.exp(source - top)
            l_ref[t, a : a + group, :] = part
            mass = mass + jnp.sum(part.reshape(group // 8, 8, TILE), axis=0)
        mass = jnp.sum(mass, axis=0, keepdims=True)
        weight = w_ref[:, where]
        chosen = act_ref[:, where]
        scale = weight / mass
        for a in range(0, actions, group):
            row = lax.broadcasted_iota(jnp.int32, (group, TILE), 0) + a
            part = l_ref[t, a : a + group, :] * scale
            part = part - jnp.where(row == chosen, weight, 0.0)
            sig_refs[a // rows][a % rows : a % rows + group, where] = part.astype(BF16)
        return carry

    lax.fori_loop(0, tiles, step, 0)


def signal_kernel(plan, segs, samples, total, here_ref, act_ref, *refs):
    pieces, refs = refs[: 2 * plan.Y], refs[2 * plan.Y :]
    n_ref, refs = refs[0], refs[1:]
    early = plan.J - 1
    known, refs = refs[: 2 * early], refs[2 * early :]
    mass_ref, norm_ref, refs = refs[0], refs[1], refs[2:]
    rest, refs = refs[:early], refs[early:]
    keep_ref, send_ref, wt_ref, w_ref, known_ref, l_ref, top_ref, sig_ref, w_sems = refs
    here = tuple(here_ref[i] for i in range(4))
    copies = fetch_policy(plan, here, early, pieces, wt_ref, w_sems)
    step_weights(plan, here, segs, samples, total, pieces, w_ref, mass_ref, norm_ref, known_ref)
    for copy in copies:
        copy.wait()
    chunk_logits(wt_ref, n_ref, l_ref, early * wt_ref.shape[0], top_ref)
    signals(known, l_ref, (sig_ref,) + tuple(rest), w_ref, act_ref, top_ref)
    gradient_chunk(plan, here, sig_ref, n_ref, keep_ref, send_ref)


def gradient_kernel(plan, here_ref, sig_ref, n_ref, keep_ref, send_ref):
    here = tuple(here_ref[i] for i in range(4))
    gradient_chunk(plan, here, sig_ref, n_ref, keep_ref, send_ref)


def chunk_shapes(plan, depth):
    shape = (plan.Y, plan.X, plan.Z, plan.block, depth)
    return [jax.ShapeDtypeStruct(shape, F32), jax.ShapeDtypeStruct(shape, BF16)]


def early_logits(plan, here, pieces, normed, count):
    tokens, width = normed.shape
    rows = count // plan.J
    return pl.pallas_call(
        functools.partial(logits_kernel, plan),
        in_specs=[SMEM] + [VMEM] * len(pieces) + [VMEM],
        out_specs=[VMEM, VMEM],
        out_shape=[
            jax.ShapeDtypeStruct((tokens // TILE, rows, TILE), F32),
            jax.ShapeDtypeStruct((tokens // TILE, 1, TILE), F32),
        ],
        scratch_shapes=[
            pltpu.VMEM((rows, width), BF16),
            pltpu.SemaphoreType.DMA((len(pieces) * plan.X * plan.Z,)),
        ],
        compiler_params=ROOM,
        cost_estimate=pl.CostEstimate(
            flops=8 * 2 * tokens * width * rows,
            bytes_accessed=1 * 2 * tokens * width + 2 * width * rows + 4 * tokens * rows,
            transcendentals=0,
        ),
        name="logits",
    )(here, *pieces, normed)


def signal_and_gradient(plan, here, actions, last, normed, known, count, segs, samples, total):
    tokens, width = normed.shape
    depth = width // plan.mp
    rows = count // plan.J
    known = [value for pair in known for value in pair]
    signal = jax.ShapeDtypeStruct((rows, tokens), BF16)
    owners = plan.C * plan.Y
    mass, norm, *rest, keep, send = pl.pallas_call(
        functools.partial(signal_kernel, plan, segs, samples, total),
        in_specs=[SMEM, VMEM] + [VMEM] * len(last) + [VMEM] + [VMEM] * len(known),
        out_specs=[SMEM] + [VMEM] * (plan.J + 2),
        out_shape=[
            jax.ShapeDtypeStruct((1, 1), F32),
            jax.ShapeDtypeStruct((owners, tokens), F32),
        ]
        + [signal] * (plan.J - 1)
        + chunk_shapes(plan, depth),
        scratch_shapes=[
            pltpu.VMEM((rows, width), BF16),
            pltpu.VMEM((1, tokens), F32),
            pltpu.VMEM((owners * plan.mp, tokens + depth), F32),
            pltpu.VMEM((tokens // TILE, count, TILE), F32),
            pltpu.VMEM((tokens // TILE, 1, TILE), F32),
            pltpu.VMEM((rows, tokens), BF16),
            pltpu.SemaphoreType.DMA((len(last) * plan.X * plan.Z,)),
        ],
        compiler_params=ROOM,
        cost_estimate=pl.CostEstimate(
            flops=4 * tokens * width * rows,
            bytes_accessed=2 * tokens * width + 2 * width * count + 6 * tokens * count,
            transcendentals=tokens * count,
        ),
        name="signal",
    )(here, actions, *last, normed, *known)
    chunks = [(keep, send)]
    for later in rest:
        chunks.append(
            pl.pallas_call(
                functools.partial(gradient_kernel, plan),
                in_specs=[SMEM, VMEM, VMEM],
                out_specs=[VMEM] * 2,
                out_shape=chunk_shapes(plan, depth),
                compiler_params=ROOM,
                cost_estimate=pl.CostEstimate(
                    flops=2 * tokens * width * rows,
                    bytes_accessed=2 * tokens * width + 2 * tokens * count,
                    transcendentals=0,
                ),
                name="gradient",
            )(here, later, normed)
        )
    return mass, norm, chunks


def assemble_kernel(plan, here_ref, *refs):
    count = 2 * plan.Y * plan.J
    pieces, updates = refs[:count], refs[count : count + 2 * plan.J]
    actor_ref, update_ref, sems = refs[-3:]
    y, c, z, x = (here_ref[i] for i in range(4))
    depth = updates[0].shape[-2]
    block = plan.block
    copies = []

    def copy(source, target):
        moved = pltpu.make_async_copy(source, target, sems.at[len(copies)])
        moved.start()
        copies.append(moved)

    for j in range(plan.J):
        for other in range(2):
            core = c ^ other
            for dy in range(plan.Y):
                col = ((j * 2 + core) * plan.Y + (y ^ dy)) * block
                copy(
                    updates[2 * j + other].at[dy],
                    update_ref.at[:, pl.ds(pl.multiple_of(col, block), block)],
                )
            for p in range(plan.Y):
                piece = pieces[(j * 2 + other) * plan.Y + p]
                for q in range(plan.X):
                    a, b = plan.relative(core, p, q)
                    for dz in range(plan.Z):
                        col = ((j * 2 + core) * plan.Y + (y ^ a)) * block
                        row = ((z ^ dz) * plan.X + (x ^ b)) * depth
                        copy(
                            piece.at[q, dz],
                            actor_ref.at[
                                pl.ds(pl.multiple_of(row, depth), depth),
                                pl.ds(pl.multiple_of(col, block), block),
                            ],
                        )
    for moved in copies:
        moved.wait()


def assemble(plan, here, pieces, updates, width, count):
    depth = width // plan.mp
    return pl.pallas_call(
        functools.partial(assemble_kernel, plan),
        in_specs=[SMEM] + [VMEM] * (len(pieces) + len(updates)),
        out_specs=[ANY] * 2,
        out_shape=[
            jax.ShapeDtypeStruct((width, count), BF16),
            jax.ShapeDtypeStruct((depth, count), F32),
        ],
        scratch_shapes=[
            pltpu.SemaphoreType.DMA((len(pieces) * plan.X * plan.Z + len(updates) * plan.Y,)),
        ],
        compiler_params=ROOM,
        name="assemble",
    )(here, *pieces, *updates)


def body(
    features,
    rewards,
    tail_value,
    actions,
    episode_ends,
    sample_owner,
    sample_row,
    norm_gain,
    value_weight,
    policy_weight,
    first_moment,
    second_moment,
):
    owners_all, columns = lax.axis_size("replay"), lax.axis_size("mp")
    segs, seg_len, width = features.shape
    depth, count = policy_weight.shape
    samples = sample_row.shape[0]
    plan = Plan(owners_all, columns, count)
    here = plan.here()
    place = (here[1] * plan.Y + here[0]).reshape(1)
    replay = lax.axis_index("replay")

    low = own_shard(plan, place, policy_weight)
    stages = [plan.gather_column(block) for block in low[:-1]]
    if stages:
        norm_gain = after(norm_gain, stages[0][1])

    asked = sample_owner[:, 0] * segs + sample_row
    normed, block = normalize(
        features.reshape(segs * seg_len, width),
        norm_gain,
        value_weight,
        rewards,
        episode_ends,
        tail_value,
        asked,
        low[-1],
    )
    column = plan.gather_column(block)
    planes = [plan.gather_plane([after(first[0], block)] + first[1:]) for first in stages]
    near = [plan.gather_near(after(plane, column[1])) for plane in planes]
    mine = plan.gather_near(plan.gather_plane(column))
    pieces = [plan.gather_far(piece) for piece in near]
    known = [early_logits(plan, here, piece, normed, count) for piece in pieces]
    pieces.append(plan.gather_far(mine))

    token_total = owners_all * columns * samples * seg_len
    total_weight, column, chunks = signal_and_gradient(
        plan, here, actions.reshape(1, -1), pieces[-1], normed, known, count, segs, samples, token_total
    )
    owner = (asked // segs) ^ replay
    slot = ((owner % plan.C) * plan.Y + owner // plan.C) * segs + asked % segs
    local_norm = column.reshape(owners_all * segs, seg_len)[slot].reshape(-1)
    fresh, updates, terms = [], [], None
    for j, (keep, send) in enumerate(chunks):
        base, low = plan.reduce(keep, send)
        if terms is not None:
            low, terms = lax.optimization_barrier((low, terms))
        terms = plan.reduce_column(low)
        update, low = own_update(
            plan, j, place, total_weight, base, terms, policy_weight, first_moment, second_moment
        )
        near = jnp.stack([update] + [plan.permute(update, "y", k) for k in range(1, plan.Y)])
        column, near = lax.optimization_barrier((plan.gather_column(low), near))
        updates += [near, plan.permute(near, "c", 1)]
        fresh += plan.gather_far(plan.gather_near(plan.gather_plane(column)))
    actor_policy, update = assemble(plan, here, fresh, updates, width, count)
    return (local_norm, update, actor_policy)


def solution(mesh):
    return jax.shard_map(
        body,
        mesh=mesh,
        in_specs=(
            P(ALL, None, None),
            P(ALL, None),
            P(ALL),
            P(ALL, None),
            P(ALL, None),
            P(ALL, None),
            P(ALL),
            P(),
            P(),
            P("mp", None),
            P("mp", None),
            P("mp", None),
        ),
        out_specs=(P(ALL), P("mp", None), P()),
        check_vma=False,
    )
```

```python
import functools

import jax
import jax.numpy as jnp
from jax import lax
from jax.experimental import pallas as pl
from jax.experimental.pallas import tpu as pltpu
from jax.sharding import PartitionSpec as P

DISCOUNT = 0.97
STEP_RATE = 0.002
ALL = ("replay", "mp")
LANES = 128
BF16 = jnp.bfloat16
F32 = jnp.float32
VMEM = pl.BlockSpec(memory_space=pltpu.VMEM)
SMEM = pl.BlockSpec(memory_space=pltpu.SMEM)
ANY = pl.BlockSpec(memory_space=pl.ANY)
HBM = pl.BlockSpec(memory_space=pltpu.HBM)
ROOM = pltpu.CompilerParams(vmem_limit_bytes=32 * 2**20)


def after(value, *others):
    return lax.optimization_barrier((value, others))[0]


class Plan:
    def __init__(self, replay, mp, actions):
        self.C = 2
        self.Y = replay // self.C
        self.Z = 4
        self.X = mp // self.Z
        self.mp = mp
        self.swap = self.X == self.Y
        self.block = LANES
        self.J = max(1, actions // (self.C * self.Y * self.block))

    def permute(self, value, axis, k):
        pairs = []
        for y in range(self.Y):
            for c in range(self.C):
                for z in range(self.Z):
                    for x in range(self.X):
                        along = axis
                        if axis in ("p", "q"):
                            along = "y" if (axis == "p") == (c == 0 or not self.swap) else "x"
                        to = dict(y=y, c=c, z=z, x=x)
                        to[along] ^= k
                        pairs.append((self.index(y, c, z, x), self.index(**to)))
        return lax.ppermute(value, ALL, pairs)

    def index(self, y, c, z, x):
        return (y * self.C + c) * self.mp + z * self.X + x

    def here(self):
        replay, mp = lax.axis_index("replay"), lax.axis_index("mp")
        return jnp.stack([replay // self.C, replay % self.C, mp // self.X, mp % self.X]).astype(jnp.int32)

    def relative(self, core, dy, dx):
        if not self.swap:
            return dy, dx
        return jnp.where(core == 0, dy, dx), jnp.where(core == 0, dx, dy)

    def gather_column(self, block):
        return [block] + [self.permute(block, "z", k) for k in range(1, self.Z)]

    def gather_plane(self, column):
        column = jnp.stack(column)
        return jnp.stack([column] + [self.permute(column, "q", k) for k in range(1, self.X)])

    def gather_near(self, plane):
        return [plane] + [self.permute(plane, "p", k) for k in range(1, self.Y)]

    def gather_far(self, mine):
        return mine + [self.permute(piece, "c", 1) for piece in mine]

    def reduce(self, keep, send):
        total = keep + self.permute(send, "c", 1).astype(F32)
        for axis in ("p", "q"):
            low = total[1:].astype(BF16)
            total = total[0]
            for k in range(1, low.shape[0] + 1):
                total = total + self.permute(low[k - 1], axis, k).astype(F32)
        return total, [total[k].astype(BF16) for k in range(1, self.Z)]

    def reduce_column(self, low):
        return [self.permute(low[k - 1], "z", k) for k in range(1, self.Z)]


def shard_kernel(plan, place_ref, w_hbm, *refs):
    outs, stage, sems = refs[: plan.J], refs[plan.J], refs[plan.J + 1]
    block = plan.block
    copies = []
    for j in range(plan.J):
        start = pl.multiple_of((j * 2 * plan.Y + place_ref[0]) * block, block)
        copy = pltpu.make_async_copy(w_hbm.at[:, pl.ds(start, block)], stage.at[j], sems.at[j])
        copy.start()
        copies.append(copy)
    for j in range(plan.J):
        copies[j].wait()
        outs[j][...] = stage[j].T.astype(BF16)


def own_shard(plan, place, policy_weight):
    depth = policy_weight.shape[0]
    block = plan.block
    return pl.pallas_call(
        functools.partial(shard_kernel, plan),
        in_specs=[SMEM, ANY],
        out_specs=[VMEM] * plan.J,
        out_shape=[jax.ShapeDtypeStruct((block, depth), BF16)] * plan.J,
        scratch_shapes=[pltpu.VMEM((plan.J, depth, block), F32), pltpu.SemaphoreType.DMA((plan.J,))],
        name="shard",
    )(place, policy_weight)


def update_kernel(count, block, first, place_ref, mass_ref, base_ref, *refs):
    terms, (w_ref, m_ref, v_ref, update_ref, low_ref) = refs[:count], refs[count:]
    own = (slice(None), pl.ds(pl.multiple_of((first + place_ref[0]) * block, block), block))
    total = base_ref[0]
    for term in terms:
        total = total + term[...].astype(F32)
    gradient = total.T / mass_ref[0, 0]
    first_new = 0.9 * m_ref[own] + 0.1 * gradient
    second_new = 0.95 * v_ref[own] + 0.05 * gradient * gradient
    update = first_new / (jnp.sqrt(second_new) + 1e-08)
    update_ref[...] = update
    low_ref[...] = (w_ref[own] - STEP_RATE * update).astype(BF16)


def own_update(plan, j, place, mass, base, terms, policy_weight, first_moment, second_moment):
    depth = policy_weight.shape[0]
    block = plan.block
    return pl.pallas_call(
        functools.partial(update_kernel, len(terms), block, j * 2 * plan.Y),
        in_specs=[SMEM, SMEM] + [VMEM] * (len(terms) + 4),
        out_specs=[VMEM, VMEM],
        out_shape=[
            jax.ShapeDtypeStruct((depth, block), F32),
            jax.ShapeDtypeStruct((depth, block), BF16),
        ],
        compiler_params=pltpu.CompilerParams(vmem_limit_bytes=16 * 2**20),
        name="update",
    )(place, mass, base, *terms, policy_weight, first_moment, second_moment)


def spread_rows(rows, lanes):
    n, steps = rows.shape
    lane = lax.broadcasted_iota(jnp.int32, (steps, lanes), 1)
    pick = (lane % steps == lax.broadcasted_iota(jnp.int32, (steps, lanes), 0)).astype(F32).astype(BF16)
    wide = jnp.dot(rows.astype(BF16), pick, preferred_element_type=F32)
    lane = lax.broadcasted_iota(jnp.int32, (n, lanes), 1)
    own = lane // steps == lax.broadcasted_iota(jnp.int32, (n, lanes), 0)
    return jnp.sum(jnp.where(own, wide, 0.0), axis=0, keepdims=True)


def norm_kernel(x_ref, gain_ref, value_ref, r_ref, e_ref, tail_ref, ask_ref, low_ref, out_ref, block_ref, val_ref):
    wide = x_ref[...].astype(F32)
    mean_square = jnp.mean(wide * wide, axis=-1, keepdims=True)
    normed = (wide * lax.rsqrt(mean_square + 1e-05) * gain_ref[...]).astype(BF16)
    out_ref[...] = normed
    tile = normed.shape[0]
    step = pl.program_id(0)
    val_ref[:, pl.ds(pl.multiple_of(step * tile, tile), tile)] = lax.dot_general(
        value_ref[...], normed, (((1,), (1,)), ((), ())), preferred_element_type=F32
    )

    @pl.when(step == pl.num_programs(0) - 1)
    def _():
        segs, seg_len = r_ref.shape
        lanes = segs * seg_len
        lane = lax.broadcasted_iota(jnp.int32, (1, lanes), 1)
        last = lane % seg_len == seg_len - 1
        ends = spread_rows(e_ref[...].astype(F32), lanes)
        tails = spread_rows(jnp.broadcast_to(tail_ref[...].astype(F32), (segs, seg_len)), lanes)
        decay = DISCOUNT * (1.0 - ends)
        total = spread_rows(r_ref[...], lanes) + jnp.where(last, decay * tails, 0.0)
        decay = jnp.where(last, 0.0, decay)
        reach = 1
        while reach < seg_len:
            total = total + decay * pltpu.roll(total, lanes - reach, axis=1)
            decay = decay * pltpu.roll(decay, lanes - reach, axis=1)
            reach *= 2
        rest = total - val_ref[0:1, :]
        block, depth = low_ref.shape
        rows = []
        for _ in range(3):
            term = rest.astype(BF16).astype(F32)
            rest = rest - term
            rows += [term[:, i : i + depth] for i in range(0, lanes, depth)]
        rows.append(ask_ref[...])
        rows.append(jnp.zeros((block_ref.shape[0] - block - len(rows), depth), F32))
        block_ref[:block, :] = low_ref[...]
        block_ref[block:, :] = jnp.concatenate(rows, axis=0).astype(BF16)


def payload_rows(lanes, depth):
    return -(-(3 * lanes // depth + 1) // 16) * 16


def normalize(rows, norm_gain, value_weight, rewards, ends, tails, asked, low):
    tokens, width = rows.shape
    tile = 256
    block, depth = low.shape
    segs = tails.shape[0]
    high = block + payload_rows(tokens, depth)
    asked = jnp.pad(asked.astype(F32)[None, :], ((0, 0), (0, depth - asked.shape[0])))

    def whole(shape):
        return pl.BlockSpec(shape, lambda i: (0, 0))

    return pl.pallas_call(
        norm_kernel,
        grid=(tokens // tile,),
        in_specs=[
            pl.BlockSpec((tile, width), lambda i: (i, 0)),
            whole((1, width)),
            whole((16, width)),
            whole(rewards.shape),
            whole(ends.shape),
            whole((segs, 1)),
            whole((1, depth)),
            whole(low.shape),
        ],
        out_specs=[pl.BlockSpec((tile, width), lambda i: (i, 0)), whole((high, depth))],
        out_shape=[
            jax.ShapeDtypeStruct((tokens, width), BF16),
            jax.ShapeDtypeStruct((high, depth), BF16),
        ],
        scratch_shapes=[pltpu.VMEM((16, tokens), F32)],
        compiler_params=pltpu.CompilerParams(vmem_limit_bytes=56 * 2**20),
        cost_estimate=pl.CostEstimate(
            flops=10 * tokens * width, bytes_accessed=4 * tokens * width, transcendentals=0
        ),
        name="normalize",
    )(
        rows,
        norm_gain.reshape(1, width),
        jnp.broadcast_to(value_weight[None, :], (16, width)),
        rewards,
        ends,
        tails.reshape(segs, 1),
        asked,
        low,
    )


def step_weights(plan, here, segs, samples, total, pieces, weight_ref, mass_ref, norm_ref, known_ref):
    lanes = weight_ref.shape[1]
    steps = lanes // segs
    owners = plan.C * plan.Y
    c = here[1]
    me = here[0] * plan.C + c
    depth = pieces[0].shape[-1]
    parts = lanes // depth
    for other in range(2):
        for dy in range(plan.Y):
            for dx in range(plan.X):
                for dz in range(plan.Z):
                    row = (other * plan.Y + dy) * plan.mp + dx * plan.Z + dz
                    sent = pieces[other * plan.Y + dy][dx, dz, plan.block :, :].astype(F32)
                    if plan.swap and dy != dx:
                        turned = pieces[other * plan.Y + dx][dy, dz, plan.block :, :].astype(F32)
                        sent = jnp.where(c == other, sent, turned)
                    value = (sent[:parts] + sent[parts : 2 * parts]) + sent[2 * parts : 3 * parts]
                    for i in range(parts):
                        known_ref[row : row + 1, i * depth : (i + 1) * depth] = value[i : i + 1]
                    known_ref[row : row + 1, lanes : lanes + depth] = sent[3 * parts : 3 * parts + 1]
    asked = known_ref[:, lanes:].astype(jnp.int32)
    owner = (asked // segs) ^ me
    slot = ((owner % plan.C) * plan.Y + owner // plan.C) * segs + asked % segs
    code = lax.broadcasted_iota(jnp.int32, (plan.mp, owners * segs), 1)
    times = jnp.zeros((plan.mp, owners * segs), F32)
    for b in range(owners):
        for i in range(samples):
            wanted = slot[b * plan.mp : (b + 1) * plan.mp, i : i + 1]
            times = times + jnp.where(code == wanted, 1.0, 0.0)
    times = times.astype(BF16)
    row = lax.broadcasted_iota(jnp.int32, (owners * segs, lanes), 0)
    lane = lax.broadcasted_iota(jnp.int32, (owners * segs, lanes), 1)
    spread_times = []
    for o in range(owners):
        pick = (row == o * segs + lane // steps).astype(F32).astype(BF16)
        spread_times.append(jnp.dot(times, pick, preferred_element_type=F32))
    times = jnp.concatenate(spread_times, axis=0)
    advantage = known_ref[:, :lanes]
    centered = advantage - jnp.sum(times * advantage) / total
    spread = jnp.sum(times * centered * centered) / total
    normalized = centered * lax.rsqrt(spread + 1e-05)
    weights = times * jnp.exp(jnp.minimum(normalized, 3.0))
    weight_ref[...] = weights[0:1, :]
    mass_ref[0, 0] = jnp.sum(weights)
    for o in range(owners):
        norm_ref[o : o + 1, :] = normalized[o * plan.mp : o * plan.mp + 1, :]


def gradient_chunk(plan, here, sig_ref, n_ref, keep_ref, send_ref):
    y, c, z, x = here
    rows = plan.Y * plan.block
    depth = keep_ref.shape[-1]
    span = plan.X * depth

    def step(plane, carry):
        part = jnp.dot(
            sig_ref[: 2 * rows, :],
            n_ref[:, pl.ds(pl.multiple_of(plane * span, span), span)],
            preferred_element_type=F32,
        )
        keep = jnp.where(c == 0, part[:rows], part[rows:])
        send = jnp.where(c == 0, part[rows:], part[:rows]).astype(BF16)
        dz = plane ^ z
        for line in range(plan.X):
            for col in range(plan.Y):
                where = (slice(col * plan.block, (col + 1) * plan.block), slice(line * depth, (line + 1) * depth))
                p, q = plan.relative(c, y ^ col, x ^ line)
                keep_ref[p, q, dz] = keep[where]
                p, q = plan.relative(1 - c, y ^ col, x ^ line)
                send_ref[p, q, dz] = send[where]
        return carry

    lax.fori_loop(0, plan.Z, step, 0)


def fetch_policy(plan, here, j, pieces, wt_ref, sems):
    y, c, z, x = here
    block = plan.block
    depth = pieces[0].shape[-1]
    copies = []
    for other in range(2):
        core = c ^ other
        for p in range(plan.Y):
            piece = pieces[other * plan.Y + p]
            for q in range(plan.X):
                a, b = plan.relative(core, p, q)
                for dz in range(plan.Z):
                    row = (core * plan.Y + (y ^ a)) * block
                    col = ((z ^ dz) * plan.X + (x ^ b)) * depth
                    copy = pltpu.make_async_copy(
                        piece.at[q, dz, 0:block],
                        wt_ref.at[
                            pl.ds(pl.multiple_of(row, block), block),
                            pl.ds(pl.multiple_of(col, depth), depth),
                        ],
                        sems.at[len(copies)],
                    )
                    copy.start()
                    copies.append(copy)
    return copies


TILE = 256


def chunk_logits(wt_ref, n_ref, l_ref, first_row, top_ref):
    rows = wt_ref.shape[0]

    def step(t, carry):
        part = lax.dot_general(
            wt_ref[...],
            n_ref[pl.ds(pl.multiple_of(t * TILE, TILE), TILE), :],
            (((1,), (1,)), ((), ())),
            preferred_element_type=F32,
        )
        l_ref[t, first_row : first_row + rows, :] = part
        top_ref[t] = jnp.max(part, axis=0, keepdims=True)
        return carry

    lax.fori_loop(0, l_ref.shape[0], step, 0)


def logits_kernel(plan, here_ref, *refs):
    pieces, refs = refs[: 2 * plan.Y], refs[2 * plan.Y :]
    n_ref, l_ref, top_ref, wt_ref, w_sems = refs
    here = tuple(here_ref[i] for i in range(4))
    copies = fetch_policy(plan, here, 0, pieces, wt_ref, w_sems)
    for copy in copies:
        copy.wait()
    chunk_logits(wt_ref, n_ref, l_ref, 0, top_ref)


def signals(known, l_ref, sig_refs, w_ref, act_ref, top_ref):
    group = 64
    tiles, actions, _ = l_ref.shape
    rows = sig_refs[0].shape[0]

    def step(t, carry):
        top = top_ref[t]
        for j in range(len(known) // 2):
            top = jnp.maximum(top, known[2 * j + 1][t])
        where = pl.ds(pl.multiple_of(t * TILE, TILE), TILE)
        mass = jnp.zeros((8, TILE), F32)
        for a in range(0, actions, group):
            j, first = a // rows, a % rows
            source = known[2 * j][t, first : first + group, :] if 2 * j < len(known) else l_ref[t, a : a + group, :]
            part = jnp.exp(source - top)
            l_ref[t, a : a + group, :] = part
            mass = mass + jnp.sum(part.reshape(group // 8, 8, TILE), axis=0)
        mass = jnp.sum(mass, axis=0, keepdims=True)
        weight = w_ref[:, where]
        chosen = act_ref[:, where]
        scale = weight / mass
        for a in range(0, actions, group):
            row = lax.broadcasted_iota(jnp.int32, (group, TILE), 0) + a
            part = l_ref[t, a : a + group, :] * scale
            part = part - jnp.where(row == chosen, weight, 0.0)
            sig_refs[a // rows][a % rows : a % rows + group, where] = part.astype(BF16)
        return carry

    lax.fori_loop(0, tiles, step, 0)


def signal_kernel(plan, segs, samples, total, here_ref, act_ref, *refs):
    pieces, refs = refs[: 2 * plan.Y], refs[2 * plan.Y :]
    n_ref, refs = refs[0], refs[1:]
    early = plan.J - 1
    known, refs = refs[: 2 * early], refs[2 * early :]
    mass_ref, norm_ref, refs = refs[0], refs[1], refs[2:]
    rest, refs = refs[:early], refs[early:]
    keep_ref, send_ref, wt_ref, w_ref, known_ref, l_ref, top_ref, sig_ref, w_sems = refs
    here = tuple(here_ref[i] for i in range(4))
    copies = fetch_policy(plan, here, early, pieces, wt_ref, w_sems)
    step_weights(plan, here, segs, samples, total, pieces, w_ref, mass_ref, norm_ref, known_ref)
    for copy in copies:
        copy.wait()
    chunk_logits(wt_ref, n_ref, l_ref, early * wt_ref.shape[0], top_ref)
    signals(known, l_ref, (sig_ref,) + tuple(rest), w_ref, act_ref, top_ref)
    gradient_chunk(plan, here, sig_ref, n_ref, keep_ref, send_ref)


def gradient_kernel(plan, here_ref, sig_ref, n_ref, keep_ref, send_ref):
    here = tuple(here_ref[i] for i in range(4))
    gradient_chunk(plan, here, sig_ref, n_ref, keep_ref, send_ref)


def chunk_shapes(plan, depth):
    shape = (plan.Y, plan.X, plan.Z, plan.block, depth)
    return [jax.ShapeDtypeStruct(shape, F32), jax.ShapeDtypeStruct(shape, BF16)]


def early_logits(plan, here, pieces, normed, count):
    tokens, width = normed.shape
    rows = count // plan.J
    return pl.pallas_call(
        functools.partial(logits_kernel, plan),
        in_specs=[SMEM] + [VMEM] * len(pieces) + [VMEM],
        out_specs=[VMEM, VMEM],
        out_shape=[
            jax.ShapeDtypeStruct((tokens // TILE, rows, TILE), F32),
            jax.ShapeDtypeStruct((tokens // TILE, 1, TILE), F32),
        ],
        scratch_shapes=[
            pltpu.VMEM((rows, width), BF16),
            pltpu.SemaphoreType.DMA((len(pieces) * plan.X * plan.Z,)),
        ],
        compiler_params=ROOM,
        cost_estimate=pl.CostEstimate(
            flops=8 * 2 * tokens * width * rows,
            bytes_accessed=1 * 2 * tokens * width + 2 * width * rows + 4 * tokens * rows,
            transcendentals=0,
        ),
        name="logits",
    )(here, *pieces, normed)


def signal_and_gradient(plan, here, actions, last, normed, known, count, segs, samples, total):
    tokens, width = normed.shape
    depth = width // plan.mp
    rows = count // plan.J
    known = [value for pair in known for value in pair]
    signal = jax.ShapeDtypeStruct((rows, tokens), BF16)
    owners = plan.C * plan.Y
    mass, norm, *rest, keep, send = pl.pallas_call(
        functools.partial(signal_kernel, plan, segs, samples, total),
        in_specs=[SMEM, VMEM] + [VMEM] * len(last) + [VMEM] + [VMEM] * len(known),
        out_specs=[SMEM] + [VMEM] * (plan.J + 2),
        out_shape=[
            jax.ShapeDtypeStruct((1, 1), F32),
            jax.ShapeDtypeStruct((owners, tokens), F32),
        ]
        + [signal] * (plan.J - 1)
        + chunk_shapes(plan, depth),
        scratch_shapes=[
            pltpu.VMEM((rows, width), BF16),
            pltpu.VMEM((1, tokens), F32),
            pltpu.VMEM((owners * plan.mp, tokens + depth), F32),
            pltpu.VMEM((tokens // TILE, count, TILE), F32),
            pltpu.VMEM((tokens // TILE, 1, TILE), F32),
            pltpu.VMEM((rows, tokens), BF16),
            pltpu.SemaphoreType.DMA((len(last) * plan.X * plan.Z,)),
        ],
        compiler_params=ROOM,
        cost_estimate=pl.CostEstimate(
            flops=4 * tokens * width * rows,
            bytes_accessed=2 * tokens * width + 2 * width * count + 6 * tokens * count,
            transcendentals=tokens * count,
        ),
        name="signal",
    )(here, actions, *last, normed, *known)
    chunks = [(keep, send)]
    for later in rest:
        chunks.append(
            pl.pallas_call(
                functools.partial(gradient_kernel, plan),
                in_specs=[SMEM, VMEM, VMEM],
                out_specs=[VMEM] * 2,
                out_shape=chunk_shapes(plan, depth),
                compiler_params=ROOM,
                cost_estimate=pl.CostEstimate(
                    flops=2 * tokens * width * rows,
                    bytes_accessed=2 * tokens * width + 2 * tokens * count,
                    transcendentals=0,
                ),
                name="gradient",
            )(here, later, normed)
        )
    return mass, norm, chunks


def assemble_kernel(plan, here_ref, *refs):
    count = 2 * plan.Y * plan.J
    pieces, updates = refs[:count], refs[count : count + 2 * plan.J]
    actor_ref, update_ref, sems = refs[-3:]
    y, c, z, x = (here_ref[i] for i in range(4))
    depth = updates[0].shape[-2]
    block = plan.block
    copies = []

    def copy(source, target):
        moved = pltpu.make_async_copy(source, target, sems.at[len(copies)])
        moved.start()
        copies.append(moved)

    for j in range(plan.J):
        for other in range(2):
            core = c ^ other
            for dy in range(plan.Y):
                col = ((j * 2 + core) * plan.Y + (y ^ dy)) * block
                copy(
                    updates[2 * j + other].at[dy],
                    update_ref.at[:, pl.ds(pl.multiple_of(col, block), block)],
                )
            for p in range(plan.Y):
                piece = pieces[(j * 2 + other) * plan.Y + p]
                for q in range(plan.X):
                    a, b = plan.relative(core, p, q)
                    for dz in range(plan.Z):
                        col = ((j * 2 + core) * plan.Y + (y ^ a)) * block
                        row = ((z ^ dz) * plan.X + (x ^ b)) * depth
                        copy(
                            piece.at[q, dz],
                            actor_ref.at[
                                pl.ds(pl.multiple_of(row, depth), depth),
                                pl.ds(pl.multiple_of(col, block), block),
                            ],
                        )
    for moved in copies:
        moved.wait()


def assemble(plan, here, pieces, updates, width, count):
    depth = width // plan.mp
    return pl.pallas_call(
        functools.partial(assemble_kernel, plan),
        in_specs=[SMEM] + [VMEM] * (len(pieces) + len(updates)),
        out_specs=[ANY] * 2,
        out_shape=[
            jax.ShapeDtypeStruct((width, count), BF16),
            jax.ShapeDtypeStruct((depth, count), F32),
        ],
        scratch_shapes=[
            pltpu.SemaphoreType.DMA((len(pieces) * plan.X * plan.Z + len(updates) * plan.Y,)),
        ],
        compiler_params=ROOM,
        name="assemble",
    )(here, *pieces, *updates)


def body(
    features,
    rewards,
    tail_value,
    actions,
    episode_ends,
    sample_owner,
    sample_row,
    norm_gain,
    value_weight,
    policy_weight,
    first_moment,
    second_moment,
):
    owners_all, columns = lax.axis_size("replay"), lax.axis_size("mp")
    segs, seg_len, width = features.shape
    depth, count = policy_weight.shape
    samples = sample_row.shape[0]
    plan = Plan(owners_all, columns, count)
    here = plan.here()
    place = (here[1] * plan.Y + here[0]).reshape(1)
    replay = lax.axis_index("replay")

    low = own_shard(plan, place, policy_weight)
    stages = [plan.gather_column(block) for block in low[:-1]]
    if stages:
        norm_gain = after(norm_gain, stages[0][1])

    asked = sample_owner[:, 0] * segs + sample_row
    normed, block = normalize(
        features.reshape(segs * seg_len, width),
        norm_gain,
        value_weight,
        rewards,
        episode_ends,
        tail_value,
        asked,
        low[-1],
    )
    column = plan.gather_column(block)
    planes = [plan.gather_plane([after(first[0], block)] + first[1:]) for first in stages]
    near = [plan.gather_near(after(plane, column[1])) for plane in planes]
    mine = plan.gather_near(plan.gather_plane(column))
    pieces = [plan.gather_far(piece) for piece in near]
    known = [early_logits(plan, here, piece, normed, count) for piece in pieces]
    pieces.append(plan.gather_far(mine))

    token_total = owners_all * columns * samples * seg_len
    total_weight, column, chunks = signal_and_gradient(
        plan, here, actions.reshape(1, -1), pieces[-1], normed, known, count, segs, samples, token_total
    )
    owner = (asked // segs) ^ replay
    slot = ((owner % plan.C) * plan.Y + owner // plan.C) * segs + asked % segs
    local_norm = column.reshape(owners_all * segs, seg_len)[slot].reshape(-1)
    fresh, updates, terms = [], [], None
    for j, (keep, send) in enumerate(chunks):
        base, low = plan.reduce(keep, send)
        if terms is not None:
            low, terms = lax.optimization_barrier((low, terms))
        terms = plan.reduce_column(low)
        update, low = own_update(
            plan, j, place, total_weight, base, terms, policy_weight, first_moment, second_moment
        )
        near = jnp.stack([update] + [plan.permute(update, "y", k) for k in range(1, plan.Y)])
        column, near = lax.optimization_barrier((plan.gather_column(low), near))
        updates += [near, plan.permute(near, "c", 1)]
        fresh += plan.gather_far(plan.gather_near(plan.gather_plane(column)))
    actor_policy, update = assemble(plan, here, fresh, updates, width, count)
    return (local_norm, update, actor_policy)


def solution(mesh):
    return jax.shard_map(
        body,
        mesh=mesh,
        in_specs=(
            P(ALL, None, None),
            P(ALL, None),
            P(ALL),
            P(ALL, None),
            P(ALL, None),
            P(ALL, None),
            P(ALL),
            P(),
            P(),
            P("mp", None),
            P("mp", None),
            P("mp", None),
        ),
        out_specs=(P(ALL), P("mp", None), P()),
        check_vma=False,
    )
```
